256 devices in a mesh: side: 2 (over core), shard: 16 (over y, z_lo), tp: 8 (over z_hi, x).
Axes of the slice: x: 4, y: 4, z: 8 (z_hi: 2, z_lo: 4; z = z_hi * 4 + z_lo), core: 2. Of those that a mesh axis runs over, the one named last changes fastest.
Arguments:
- tokens: bfloat16 [32, 4096], P(None, 'shard'), may hold values from -24 to 24
- lengths: int32 [32], replicated, may hold values from 1 to 4096, as said below
- kv_cache: bfloat16 [2, 32, 4096, 8, 256], P('side', 'shard', None, 'tp'), may hold values from -104 to 104
- attn_gain: float32 [2, 4096], P('side', 'shard'), may hold values from 0.1 to 1.9
- qkv_weight: bfloat16 [2, 4096, 8, 768], P('side', 'shard', 'tp'), may hold values from -0.09375 to 0.09375
- out_weight: bfloat16 [2, 8, 512, 4096], P('side', 'tp', None, 'shard'), may hold values from -0.25 to 0.25
- ffn_gain: float32 [2, 4096], P('side', 'shard'), may hold values from 0.1 to 1.9
- gate_up: bfloat16 [2, 4096, 2, 14336], P('side', 'shard', None, 'tp'), may hold values from -0.09375 to 0.09375
- down_weight: bfloat16 [2, 14336, 4096], P('side', 'tp', 'shard'), may hold values from -0.046875 to 0.046875
Outputs:
- streams: bfloat16 [2, 32, 4096], P('side', None, 'shard')
- row_scales: float32 [2, 2, 32], P('side')
The draws below stay inside these ranges and needn't reach their ends.
Inputs may be any that keep to these rules, and one draw needn't show every extreme that they name: `lengths`: some sequence has exactly 4096 cached positions.
All inputs are finite; a program needn't handle non-finite values.
Results may differ from the reference program's by a relative error of at most 0.03.
Values may be sent and summed in bfloat16 or wider, within the bound.
A program may use at most 64 MiB of HBM per device.

```python
import math
import jax
import jax.numpy as jnp
from jax import lax

D = 4096
FF = 14336
H = 32
KVH = 8
HD = 128
SEQS = 32
CTX = 4096
GROUP = 4


def draw_tokens(key, part):
    key = jax.random.fold_in(key, 11)
    base_key, row_key, column_key = jax.random.split(key, 3)
    row_scale = jnp.exp(jax.random.uniform(row_key, (SEQS, 1), jnp.float32, math.log(0.05), math.log(0.5)))
    column_scale = jnp.exp(jax.random.uniform(column_key, (1, D), jnp.float32, math.log(0.4), math.log(2.4)))
    place = jnp.arange(D, dtype=jnp.float32)[None, :] / D
    column_scale = column_scale * jnp.sqrt(1.0 + 4.0 * place)
    values = jax.random.normal(base_key, (SEQS, D), jnp.float32)
    return jnp.clip(values * row_scale * column_scale, -24.0, 24.0).astype(jnp.bfloat16)


def draw_lengths(key, part):
    key = jax.random.fold_in(key, 5)
    first_key, second_key, order_key, short_key = jax.random.split(key, 4)
    first_draw = jax.random.randint(first_key, (SEQS,), 1, CTX + 1)
    second_draw = jax.random.randint(second_key, (SEQS,), 1, CTX + 1)
    short_draw = jax.random.randint(short_key, (SEQS,), 1, 5)
    order = jax.random.permutation(order_key, SEQS)
    shorter = jnp.minimum(first_draw, second_draw)
    chosen = jnp.where(order < SEQS // 4, short_draw, shorter)
    return jnp.where(order == SEQS - 1, CTX, chosen).astype(jnp.int32)


def draw_kv_cache(key, part):
    key = jax.random.fold_in(key, 7)
    base_key = jax.random.fold_in(key, 0)
    shape_all = (2, SEQS, CTX, KVH, 2 * HD)
    values = jnp.clip(jax.random.normal(base_key, shape_all, jnp.float32), -6.0, 6.0)
    return values.astype(jnp.bfloat16)


def draw_out_weight(key, part):
    key = jax.random.fold_in(key, 13)
    base_key, level_key = jax.random.split(key, 2)
    levels = jnp.exp(jax.random.uniform(level_key, (2, 1, 1, 16), jnp.float32, -1.5, 1.5))
    column_block = jnp.arange(D, dtype=jnp.int32) * 16 // D
    column_level = jnp.take(levels, column_block, axis=3)
    values = jnp.clip(jax.random.normal(base_key, (2, KVH, GROUP * HD, D), jnp.float32), -4.0, 4.0)
    values = values * (1.0 / math.sqrt(H * HD)) * column_level
    return jnp.clip(values, -0.25, 0.25).astype(jnp.bfloat16)


def block_levels(key, shape, shards, smallest, top_value):
    def one(axis_at, parts):
        heights = jax.random.uniform(jax.random.fold_in(jax.random.fold_in(key, 6), axis_at), (parts,), jnp.float32, smallest / len(shards), top_value / len(shards))
        return jnp.repeat(jnp.exp(heights), shape[axis_at] // parts).reshape((-1,) + (1,) * (len(shape) - axis_at - 1))

    level = one(*shards[0])
    for cut in shards[1:]:
        level = level * one(*cut)
    return level


def bell_draw(key, dims, spread, most, cuts=(), held_as=jnp.bfloat16):
    factor_of = block_levels(key, dims, cuts, -0.22, 0.18) if cuts else 1.0
    drawn = jax.random.normal(key, dims, jnp.float32) * spread * factor_of
    return jnp.minimum(jnp.maximum(drawn, -most), most).astype(held_as)


def setup_inputs(seed: int = 0) -> dict:
    splits = jax.random.split(jax.random.key(seed), 10)
    return {
        "tokens": draw_tokens(jax.random.fold_in(splits[9], 71), 0),
        "lengths": draw_lengths(jax.random.fold_in(splits[9], 71), 0),
        "kv_cache": draw_kv_cache(jax.random.fold_in(splits[9], 71), 0),
        "attn_gain": jnp.clip(1.0 + 0.18 * jax.random.normal(splits[3], (2, D), jnp.float32), 0.1, 1.9),
        "qkv_weight": bell_draw(splits[4], (2, D, KVH, (GROUP + 2) * HD), D ** -0.5, 0.09375, ((0, 2), (1, 16), (2, 8))),
        "out_weight": draw_out_weight(jax.random.fold_in(splits[9], 71), 0),
        "ffn_gain": jnp.clip(1.0 + 0.18 * jax.random.normal(splits[6], (2, D), jnp.float32), 0.1, 1.9),
        "gate_up": bell_draw(splits[7], (2, D, 2, FF), D ** -0.5, 0.09375, ((0, 2), (1, 16), (3, 8))),
        "down_weight": bell_draw(splits[8], (2, FF, D), FF ** -0.5, 0.046875, ((0, 2), (1, 8), (2, 16))),
    }


EPSILON = 1e-05
ROPE_BASE = 500000.0

def rms_scale(stream, gain_row):
    values = stream.astype(jnp.float32)
    mean_square = lax.optimization_barrier(jnp.mean(values * values, axis=-1))
    factor = lax.rsqrt(mean_square + EPSILON)
    return ((values * factor[:, None] * gain_row).astype(jnp.bfloat16), factor)

def rotate(vectors, positions):
    half_dim = vectors.shape[-1] // 2
    freqs = ROPE_BASE ** (-jnp.arange(half_dim, dtype=jnp.float32) * 2.0 / vectors.shape[-1])
    angles = positions.astype(jnp.float32)[:, None] * freqs[None, :]
    shape_out = (angles.shape[0],) + (1,) * (vectors.ndim - 2) + (half_dim,)
    cosine = jnp.cos(angles).reshape(shape_out)
    sine = jnp.sin(angles).reshape(shape_out)
    lower = vectors[..., :half_dim]
    upper = vectors[..., half_dim:]
    return jnp.concatenate([lower * cosine - upper * sine, upper * cosine + lower * sine], axis=-1)

def attention_layer(stream, cache, qkv_part, out_part, gain_row, lengths):
    seq_count = stream.shape[0]
    normed, factor = rms_scale(stream, gain_row)
    mixed = jnp.dot(normed, qkv_part.reshape(qkv_part.shape[0], -1), preferred_element_type=jnp.float32)
    mixed = mixed.reshape(seq_count, KVH, GROUP + 2, HD)
    queries = rotate(mixed[:, :, :GROUP], lengths).astype(jnp.bfloat16)
    new_keys = rotate(mixed[:, :, GROUP], lengths).astype(jnp.bfloat16)
    new_values = mixed[:, :, GROUP + 1].astype(jnp.bfloat16)

    def per_head(inputs):
        head_queries, head_cache, head_keys, head_values = inputs
        query_f32 = head_queries.astype(jnp.float32)
        cache_keys = head_cache[..., :HD].astype(jnp.float32)
        cache_values = head_cache[..., HD:].astype(jnp.float32)
        scores = jnp.einsum('sgh,sth->sgt', query_f32, cache_keys) * HD ** (-0.5)
        valid_mask = jnp.arange(CTX)[None, None, :] < lengths[:, None, None]
        own_score = jnp.einsum('sgh,sh->sg', query_f32, head_keys.astype(jnp.float32)) * HD ** (-0.5)
        row_top = jnp.maximum(lax.optimization_barrier(jnp.max(jnp.where(valid_mask, scores, -jnp.inf), axis=-1)), own_score)
        weights = jnp.where(valid_mask, jnp.exp(scores - row_top[..., None]), 0.0)
        own_weight = jnp.exp(own_score - row_top)
        row_total = lax.optimization_barrier(jnp.sum(weights, axis=-1)) + own_weight
        rounded = lax.optimization_barrier(weights.astype(jnp.bfloat16)).astype(jnp.float32)
        own_rounded = lax.optimization_barrier(own_weight.astype(jnp.bfloat16)).astype(jnp.float32)
        mixed_values = jnp.einsum('sgt,sth->sgh', rounded, cache_values)
        mixed_values = mixed_values + own_rounded[..., None] * head_values.astype(jnp.float32)[:, None, :]
        return (mixed_values / row_total[..., None]).astype(jnp.bfloat16)
    heads_out = lax.map(per_head, (jnp.moveaxis(queries, 1, 0), jnp.moveaxis(cache, 2, 0), jnp.moveaxis(new_keys, 1, 0), jnp.moveaxis(new_values, 1, 0)))
    attended = jnp.moveaxis(heads_out, 0, 1).reshape(seq_count, -1)
    projected = jnp.dot(attended, out_part.reshape(-1, out_part.shape[-1]), preferred_element_type=jnp.float32)
    return ((stream.astype(jnp.float32) + projected).astype(jnp.bfloat16), factor)

def ffn_layer(stream, gain_row, gate_part, down_part):
    seq_count = stream.shape[0]
    normed, factor = rms_scale(stream, gain_row)
    both = jnp.dot(normed, gate_part.reshape(gate_part.shape[0], -1), preferred_element_type=jnp.float32)
    both = both.reshape(seq_count, 2, FF)
    hidden_rows = (jax.nn.silu(both[:, 0]) * both[:, 1]).astype(jnp.bfloat16)
    projected = jnp.dot(hidden_rows, down_part, preferred_element_type=jnp.float32)
    return ((stream.astype(jnp.float32) + projected).astype(jnp.bfloat16), factor)

def reference(tokens, lengths, kv_cache, attn_gain, qkv_weight, out_weight, ffn_gain, gate_up, down_weight):
    attended, attn_one = attention_layer(tokens, kv_cache[0], qkv_weight[0], out_weight[0], attn_gain[0], lengths)
    first, ffn_one = ffn_layer(attended, ffn_gain[1], gate_up[1], down_weight[1])
    attended, attn_two = attention_layer(first, kv_cache[1], qkv_weight[1], out_weight[1], attn_gain[1], lengths)
    second, ffn_two = ffn_layer(attended, ffn_gain[0], gate_up[0], down_weight[0])
    scales = jnp.stack([jnp.stack([attn_one, ffn_two]), jnp.stack([attn_two, ffn_one])])
    return (jnp.stack([second, first]), scales)
```

```python
import functools

import jax
import jax.numpy as jnp
import numpy as np
from jax import lax
from jax.experimental import pallas as pl
from jax.experimental.pallas import tpu as pltpu
from jax.sharding import PartitionSpec as P

D = 4096
HD = 128
ROWS = 32
EPSILON = 1e-05
ROPE_BASE = 500000.0
SHARDS = 16
TPS = 8
TILES = 14
CTX = 4096
BF = jnp.bfloat16
F32 = jnp.float32


def nt_dot(a, b):
    return lax.dot_general(a, b, (((1,), (1,)), ((), ())), preferred_element_type=F32)


def wait_bytes(ref, sem):
    pltpu.make_async_copy(ref, ref, sem).wait()


def kernel(
    tok_ref, lens_ref, again_ref, fgain_ref, freq_ref, cache_hbm, wqkv_hbm, wout_hbm, wgu_hbm, wdn_hbm,
    out_ref, scale_ref,
    kbuf, vbuf, wqkv, wout, graw, wgu, wdn,
    x_buf, a_buf, resid,
    ss_send, ss_recv, stage, send1, recv1, send2, recv2, heads_f32,
    send3, recv3, send4, recv4, send5, recv5, send6, recv6,
    load_sem, gu_sem, ss_send_sem, ss_recv_sem, send_sem, recv_sem, res_sem,
):
    side = lax.axis_index("side")
    s = lax.axis_index("shard")
    t = lax.axis_index("tp")

    def shard_peer(d):
        return lax.rem(s + d, SHARDS)

    def tp_peer(d):
        return lax.rem(t + d, TPS)

    def remote(src, dst, ssem, rsem, device):
        return pltpu.make_async_remote_copy(
            src_ref=src, dst_ref=dst, send_sem=ssem, recv_sem=rsem, device_id=device,
            device_id_type=pl.DeviceIdType.MESH,
        )

    loads = [pltpu.make_async_copy(wqkv_hbm, wqkv, load_sem.at[0])]
    for i in range(2):
        loads.append(pltpu.make_async_copy(
            cache_hbm.at[i, :, pl.ds(0, HD)], kbuf.at[:, pl.ds(HD * i, HD)], load_sem.at[1 + i]))
        loads.append(pltpu.make_async_copy(
            cache_hbm.at[i, :, pl.ds(HD, HD)], vbuf.at[:, pl.ds(HD * i, HD)], load_sem.at[3 + i]))
    loads.append(pltpu.make_async_copy(wout_hbm, wout, load_sem.at[5]))
    loads.append(pltpu.make_async_copy(wdn_hbm, wdn, load_sem.at[6]))
    for load in loads:
        load.start()
    gu_loads = [
        pltpu.make_async_copy(wgu_hbm.at[:, :, pl.ds(HD * j, HD)], graw.at[j], gu_sem.at[j]) for j in range(TILES)
    ]
    for load in gu_loads:
        load.start()

    barrier = pltpu.get_barrier_semaphore()

    def greet(device):
        pl.semaphore_signal(barrier, inc=1, device_id=device, device_id_type=pl.DeviceIdType.MESH)

    def greet_shard(d, carry):
        greet((side, shard_peer(d), t))
        return carry

    def greet_tp(d, carry):
        greet((side, s, tp_peer(d)))
        return carry

    def greet_other(d, carry):
        greet((1 - side, s, tp_peer(d)))
        return carry

    lax.fori_loop(1, SHARDS, greet_shard, 0)
    lax.fori_loop(1, TPS, greet_tp, 0)
    lax.fori_loop(0, TPS, greet_other, 0)

    stage[...] = jnp.zeros_like(stage)
    x_buf[...] = tok_ref[...]
    diagonal = lax.broadcasted_iota(jnp.int32, (ROWS, HD), 0) == lax.broadcasted_iota(jnp.int32, (ROWS, HD), 1)
    pl.semaphore_wait(barrier, SHARDS - 1 + 2 * TPS - 1)

    def share_squares(values, which):
        column = jnp.sum(values * values, axis=1, keepdims=True)
        row = jnp.sum(jnp.where(diagonal, column, 0.0), axis=0, keepdims=True)
        ss_send[which] = row
        ss_recv[which, s] = row

        def go(d, carry):
            remote(ss_send.at[which], ss_recv.at[which, s], ss_send_sem.at[which], ss_recv_sem.at[which],
                   (side, shard_peer(d), t)).start()
            return carry

        lax.fori_loop(1, SHARDS, go, 0)

    def squares_factor(which):
        wait_bytes(ss_recv.at[which, pl.ds(0, SHARDS - 1)], ss_recv_sem.at[which])
        total = jnp.sum(ss_recv[which], axis=0)
        factor = lax.rsqrt(total / D + EPSILON)
        scale_ref[pl.ds(which, 1), :] = factor[:, :ROWS]
        return factor

    def attention():
        values = x_buf[...].astype(F32)
        share_squares(values, 0)
        scaled = (values * again_ref[...]).astype(BF)
        loads[0].wait()
        mixed = jnp.dot(scaled, wqkv[...], preferred_element_type=F32)
        for part in range(6):
            stage[pl.ds(part, ROWS, stride=8), :] = mixed[:, HD * part:HD * (part + 1)]
        send1[...] = stage[...].astype(BF)
        recv1[s] = send1[pl.ds(pl.multiple_of(16 * s, 16), 16), :]

        def go1(d, carry):
            to = shard_peer(d)
            remote(send1.at[pl.ds(pl.multiple_of(16 * to, 16), 16)], recv1.at[s], send_sem.at[0], recv_sem.at[0],
                   (side, to, t)).start()
            return carry

        lax.fori_loop(1, SHARDS, go1, 0)

        lens = [lens_ref[2 * s + i] for i in range(2)]
        lane = lax.broadcasted_iota(jnp.int32, (1, HD), 1)
        upper_row = lax.broadcasted_iota(jnp.int32, (16, 1), 0) >= 8
        position = jnp.where(upper_row, lens[1], lens[0])
        angle = position.astype(F32) * freq_ref[...]
        cosine = jnp.cos(angle)
        sine = jnp.where(lane < HD // 2, -jnp.sin(angle), jnp.sin(angle))

        factor = squares_factor(0)
        own_factor = jnp.sum(
            jnp.where(lane == jnp.where(upper_row, 2 * s + 1, 2 * s), factor, 0.0), axis=1, keepdims=True)
        wait_bytes(recv1.at[pl.ds(0, SHARDS - 1)], recv_sem.at[0])
        own = jnp.sum(recv1[...].astype(F32), axis=0) * own_factor
        rotated = own * cosine + pltpu.roll(own, HD // 2, 1) * sine
        rotated = rotated.astype(BF).astype(F32)
        own_values = own.astype(BF).astype(F32)
        new_key = jnp.concatenate(
            [jnp.broadcast_to(rotated[8 * i + 4:8 * i + 5], (8, HD)) for i in range(2)], axis=0)
        new_value = jnp.concatenate(
            [jnp.broadcast_to(own_values[8 * i + 5:8 * i + 6], (8, HD)) for i in range(2)], axis=0)
        own_score = jnp.sum(rotated * new_key, axis=1, keepdims=True) * HD ** (-0.5)
        both = jnp.concatenate(
            [jnp.where(upper_row, 0.0, rotated), jnp.where(upper_row, rotated, 0.0)], axis=1).astype(BF)
        loads[1].wait()
        loads[3].wait()
        scores = nt_dot(both, kbuf[...]) * HD ** (-0.5)
        at = lax.broadcasted_iota(jnp.int32, (16, CTX), 1)
        scores = jnp.where(at < position, scores, -1e30)
        top = jnp.maximum(jnp.max(scores, axis=1, keepdims=True), own_score)
        weights = jnp.exp(scores - top)
        own_weight = jnp.exp(own_score - top)
        total = jnp.sum(weights, axis=1, keepdims=True) + own_weight
        loads[2].wait()
        loads[4].wait()
        mixed_values = jnp.dot(weights.astype(BF), vbuf[...], preferred_element_type=F32)
        mixed_values = jnp.concatenate([mixed_values[:8, :HD], mixed_values[8:, HD:]], axis=0)
        mixed_values = mixed_values + own_weight.astype(BF).astype(F32) * new_value
        heads = (mixed_values / total).astype(BF)
        send2[...] = heads
        recv2[s] = heads

        def go2(d, carry):
            remote(send2, recv2.at[s], send_sem.at[1], recv_sem.at[1], (side, shard_peer(d), t)).start()
            return carry

        lax.fori_loop(1, SHARDS, go2, 0)
        loads[5].wait()
        wait_bytes(recv2.at[pl.ds(0, SHARDS - 1)], recv_sem.at[1])
        heads_f32[...] = recv2[...].astype(F32).reshape(16 * SHARDS, HD)
        gathered = jnp.concatenate(
            [heads_f32[pl.ds(g, ROWS, stride=8), :] for g in range(4)], axis=1).astype(BF)
        send3[...] = jnp.dot(gathered, wout[...], preferred_element_type=F32).astype(BF)

        def go3(d, carry):
            remote(send3, recv3.at[t], send_sem.at[2], recv_sem.at[2], (1 - side, s, tp_peer(d))).start()
            return carry

        lax.fori_loop(0, TPS, go3, 0)

    def prepare():
        for load in gu_loads:
            load.wait()
        out_row = lax.broadcasted_iota(jnp.int32, (512, 512), 0)
        in_row = lax.broadcasted_iota(jnp.int32, (512, 512), 1)
        wanted = jnp.where(out_row < 256, 2 * out_row, 2 * (out_row - 256) + 1)
        pick = jnp.where(in_row == wanted, 1.0, 0.0).astype(BF)

        def one(j, carry):
            apart = jnp.dot(pick, graw[j].reshape(512, HD), preferred_element_type=F32).astype(BF)
            wgu[j] = jnp.concatenate([apart[:256], apart[256:]], axis=1)
            return carry

        lax.fori_loop(0, TILES, one, 0)

    def feed_forward():
        prepare()

        @pl.when(side == 1)
        def _():
            resid[...] = tok_ref[...]

        @pl.when(side == 0)
        def _():
            wait_bytes(resid, res_sem.at[1])

        wait_bytes(recv3, recv_sem.at[2])
        after = (resid[...].astype(F32) + jnp.sum(recv3[...].astype(F32), axis=0)).astype(BF)
        a_buf[...] = after
        values = after.astype(F32)
        share_squares(values, 1)
        scaled = (values * fgain_ref[...]).astype(BF)

        def tile(j, carry):
            send4[j] = jnp.dot(scaled, wgu[j], preferred_element_type=F32).astype(BF)
            return carry

        lax.fori_loop(0, TILES, tile, 0)

        @pl.when(s < TILES)
        def _():
            recv4[s] = send4[s]

        def go4(d, carry):
            to = shard_peer(d)

            @pl.when(to < TILES)
            def _():
                remote(send4.at[to], recv4.at[s], send_sem.at[3], recv_sem.at[3], (side, to, t)).start()

            return carry

        lax.fori_loop(1, SHARDS, go4, 0)
        factor = squares_factor(1)
        column = jnp.sum(jnp.where(diagonal, factor, 0.0), axis=1, keepdims=True)

        @pl.when(s < TILES)
        def _():
            wait_bytes(recv4.at[pl.ds(0, SHARDS - 1)], recv_sem.at[3])
            both = jnp.sum(recv4[...].astype(F32), axis=0) * column
            gate, up = both[:, :HD], both[:, HD:]
            hidden = (gate / (1.0 + jnp.exp(-gate)) * up).astype(BF)
            send5[...] = hidden
            recv5[s] = hidden

            def go5(d, carry):
                remote(send5, recv5.at[s], send_sem.at[4], recv_sem.at[4], (side, shard_peer(d), t)).start()
                return carry

            lax.fori_loop(1, SHARDS, go5, 0)

        loads[6].wait()

        @pl.when(s < TILES)
        def _():
            wait_bytes(recv5.at[pl.ds(0, TILES - 1)], recv_sem.at[4])

        @pl.when(s >= TILES)
        def _():
            wait_bytes(recv5, recv_sem.at[4])

        hidden_all = jnp.concatenate([recv5[j] for j in range(TILES)], axis=1)
        partial = jnp.dot(hidden_all, wdn[...], preferred_element_type=F32).astype(BF)
        send6[...] = partial
        recv6[t] = partial

        def go6(d, carry):
            remote(send6, recv6.at[t], send_sem.at[5], recv_sem.at[5], (side, s, tp_peer(d))).start()
            return carry

        lax.fori_loop(1, TPS, go6, 0)
        wait_bytes(recv6.at[pl.ds(0, TPS - 1)], recv_sem.at[5])
        result = (a_buf[...].astype(F32) + jnp.sum(recv6[...].astype(F32), axis=0)).astype(BF)
        out_ref[...] = result

        @pl.when(side == 1)
        def _():
            x_buf[...] = result
            remote(x_buf, resid, res_sem.at[0], res_sem.at[1], (0, s, t)).start()

    pl.when(side == 0)(attention)
    feed_forward()
    pl.when(side == 1)(attention)

    for which in range(2):
        wait_bytes(ss_recv.at[which, pl.ds(0, SHARDS - 1)], ss_send_sem.at[which])
    wait_bytes(recv1.at[pl.ds(0, SHARDS - 1)], send_sem.at[0])
    wait_bytes(recv2.at[pl.ds(0, SHARDS - 1)], send_sem.at[1])
    wait_bytes(recv3, send_sem.at[2])

    @pl.when(s < TILES)
    def _():
        wait_bytes(recv4.at[pl.ds(0, TILES - 1)], send_sem.at[3])
        wait_bytes(recv2_like(recv5_full=recv4, rows=SHARDS - 1), send_sem.at[4])

    @pl.when(s >= TILES)
    def _():
        wait_bytes(recv4.at[pl.ds(0, TILES)], send_sem.at[3])

    wait_bytes(recv6.at[pl.ds(0, TPS - 1)], send_sem.at[5])

    @pl.when(side == 1)
    def _():
        wait_bytes(x_buf, res_sem.at[0])


def recv2_like(recv5_full, rows):
    return recv5_full.at[pl.ds(0, rows), :, pl.ds(0, HD)]


def body(tokens, lengths, kv_cache, attn_gain, qkv_weight, out_weight, ffn_gain, gate_up, down_weight):
    freqs = (ROPE_BASE ** (-np.arange(HD // 2, dtype=np.float64) * 2.0 / HD)).astype(np.float32)
    freqs = jnp.asarray(np.concatenate([freqs, freqs])[None])
    vmem = pl.BlockSpec(memory_space=pltpu.VMEM)
    smem = pl.BlockSpec(memory_space=pltpu.SMEM)
    hbm = pl.BlockSpec(memory_space=pl.ANY)
    out, scales = pl.pallas_call(
        kernel,
        out_shape=(jax.ShapeDtypeStruct((ROWS, 256), BF), jax.ShapeDtypeStruct((2, ROWS), F32)),
        in_specs=[vmem, smem, vmem, vmem, vmem, hbm, hbm, hbm, hbm, hbm],
        out_specs=(vmem, vmem),
        scratch_shapes=[
            pltpu.VMEM((CTX, 2 * HD), BF), pltpu.VMEM((CTX, 2 * HD), BF),
            pltpu.VMEM((256, 768), BF), pltpu.VMEM((512, 256), BF),
            pltpu.VMEM((TILES, 256, 2, HD), BF), pltpu.VMEM((TILES, 256, 2 * HD), BF),
            pltpu.VMEM((TILES * HD, 256), BF),
            pltpu.VMEM((ROWS, 256), BF), pltpu.VMEM((ROWS, 256), BF), pltpu.VMEM((ROWS, 256), BF),
            pltpu.VMEM((2, 1, HD), F32), pltpu.VMEM((2, SHARDS, 1, HD), F32),
            pltpu.VMEM((16 * SHARDS, HD), F32), pltpu.VMEM((16 * SHARDS, HD), BF),
            pltpu.VMEM((SHARDS, 16, HD), BF),
            pltpu.VMEM((16, HD), BF), pltpu.VMEM((SHARDS, 16, HD), BF), pltpu.VMEM((16 * SHARDS, HD), F32),
            pltpu.VMEM((ROWS, 256), BF), pltpu.VMEM((TPS, ROWS, 256), BF),
            pltpu.VMEM((TILES, ROWS, 256), BF), pltpu.VMEM((SHARDS, ROWS, 256), BF),
            pltpu.VMEM((ROWS, HD), BF), pltpu.VMEM((TILES, ROWS, HD), BF),
            pltpu.VMEM((ROWS, 256), BF), pltpu.VMEM((TPS, ROWS, 256), BF),
            pltpu.SemaphoreType.DMA((7,)), pltpu.SemaphoreType.DMA((TILES,)),
            pltpu.SemaphoreType.DMA((2,)), pltpu.SemaphoreType.DMA((2,)),
            pltpu.SemaphoreType.DMA((6,)), pltpu.SemaphoreType.DMA((6,)), pltpu.SemaphoreType.DMA((2,)),
        ],
        compiler_params=pltpu.CompilerParams(
            collective_id=0, has_side_effects=True, vmem_limit_bytes=48 * 1024 * 1024),
        cost_estimate=pl.CostEstimate(flops=130_000_000, bytes_accessed=7_500_000, transcendentals=70_000),
    )(
        tokens, lengths, attn_gain, ffn_gain, freqs,
        kv_cache.reshape(2, CTX, 2 * HD), qkv_weight.reshape(256, 768), out_weight.reshape(512, 256),
        gate_up.reshape(256, 2, 1792), down_weight.reshape(1792, 256),
    )
    return (out[None], scales[None])


def solution(mesh):
    in_specs = (
        P(None, "shard"),
        P(),
        P("side", "shard", None, "tp", None),
        P("side", "shard"),
        P("side", "shard", "tp", None),
        P("side", "tp", None, "shard"),
        P("side", "shard"),
        P("side", "shard", None, "tp"),
        P("side", "tp", "shard"),
    )
    out_specs = (P("side", None, "shard"), P("side", None, None))
    return jax.shard_map(body, mesh=mesh, in_specs=in_specs, out_specs=out_specs, check_vma=False)
```

```python
import jax
import jax.numpy as jnp
import numpy as np
from jax import lax
from jax.experimental import pallas as pl
from jax.experimental.pallas import tpu as pltpu
from jax.sharding import PartitionSpec as P

D = 4096
HD = 128
ROWS = 32
EPSILON = 1e-05
ROPE_BASE = 500000.0
SHARDS = 16
TPS = 8
TILES = 14
OWNERS = 7
CTX = 4096
BF = jnp.bfloat16
F32 = jnp.float32
MESH = pl.DeviceIdType.MESH


def nt_dot(a, b):
    return lax.dot_general(a, b, (((1,), (1,)), ((), ())), preferred_element_type=F32)


def wait_bytes(ref, sem):
    pltpu.make_async_copy(ref, ref, sem).wait()


def remote(src, dst, ssem, rsem, device):
    return pltpu.make_async_remote_copy(
        src_ref=src, dst_ref=dst, send_sem=ssem, recv_sem=rsem, device_id=device, device_id_type=MESH)


def kernel(
    tok_hbm, lens_hbm, again_hbm, fgain_hbm, freq_hbm, cache_hbm, wqkv_hbm, wout_hbm, wgu_hbm, wdn_hbm,
    out_ref, scale_ref,
    lens, again, fgain, freq,
    kbuf, vbuf, wqkv, wout, graw, wgu, wdn,
    x_buf, a_buf,
    ss_send, ss_recv, stage, send1, recv1, send2, recv2, heads_f32,
    send3, recv3, send4, recv4, send5, recv5, send6, recv6, end_buf, end_scale,
    load_sem, gu_sem, ss_send_sem, ss_recv_sem, send1_sem, recv1_sem, send2_sem, recv2_sem,
    send_sem, recv_sem, push_send, push_recv, end_send, end_recv,
):
    side = lax.axis_index("side")
    s = lax.axis_index("shard")
    t = lax.axis_index("tp")
    mate = (1 - side, s, t)

    def shard_peer(d):
        return lax.rem(s + d, SHARDS)

    def tp_peer(d):
        return lax.rem(t + d, TPS)

    barrier = pltpu.get_barrier_semaphore()

    def greet(device):
        pl.semaphore_signal(barrier, inc=1, device_id=device, device_id_type=MESH)

    def loop(start, stop, step):
        def go(d, carry):
            step(d)
            return carry

        lax.fori_loop(start, stop, go, 0)

    @pl.when(side == 0)
    def _():
        loop(1, SHARDS, lambda d: greet((0, shard_peer(d), t)))
        greet(mate)

    @pl.when(side == 1)
    def _():
        loop(0, SHARDS, lambda d: greet((0, shard_peer(d), t)))
        loop(1, SHARDS, lambda d: greet((1, shard_peer(d), t)))
        loop(1, TPS, lambda d: greet((1, s, tp_peer(d))))

    first_loads = [
        pltpu.make_async_copy(tok_hbm, x_buf, load_sem.at[0]),
        pltpu.make_async_copy(again_hbm, again, load_sem.at[1]),
        pltpu.make_async_copy(wqkv_hbm, wqkv, load_sem.at[2]),
        pltpu.make_async_copy(lens_hbm, lens, load_sem.at[3]),
        pltpu.make_async_copy(freq_hbm, freq, load_sem.at[4]),
    ]
    cache_loads = []
    for i in range(2):
        cache_loads.append(pltpu.make_async_copy(
            cache_hbm.at[i, :, pl.ds(0, HD)], kbuf.at[:, pl.ds(HD * i, HD)], load_sem.at[5 + i]))
        cache_loads.append(pltpu.make_async_copy(
            cache_hbm.at[i, :, pl.ds(HD, HD)], vbuf.at[:, pl.ds(HD * i, HD)], load_sem.at[7 + i]))
    own_loads = [
        pltpu.make_async_copy(fgain_hbm, fgain.at[0], load_sem.at[9]),
        pltpu.make_async_copy(wdn_hbm, wdn.at[0], load_sem.at[10]),
        pltpu.make_async_copy(wout_hbm, wout.at[1], load_sem.at[11]),
    ]
    gu_loads = [
        pltpu.make_async_copy(wgu_hbm.at[:, :, pl.ds(HD * j, HD)], graw.at[j], gu_sem.at[j]) for j in range(TILES)
    ]
    for load in first_loads:
        load.start()

    @pl.when(side == 0)
    def _():
        for load in cache_loads:
            load.start()

    for load in gu_loads:
        load.start()

    @pl.when(side == 1)
    def _():
        for load in own_loads:
            load.start()
        for load in cache_loads:
            load.start()

    pushes = [
        remote(wout_hbm, wout.at[0], push_send.at[0], push_recv.at[0], mate),
        remote(fgain_hbm, fgain.at[1], push_send.at[1], push_recv.at[1], mate),
        remote(wdn_hbm, wdn.at[1], push_send.at[2], push_recv.at[2], mate),
        remote(wgu.at[1], wgu.at[1], push_send.at[3], push_recv.at[3], mate),
    ]

    stage[...] = jnp.zeros_like(stage)
    diagonal = lax.broadcasted_iota(jnp.int32, (ROWS, HD), 0) == lax.broadcasted_iota(jnp.int32, (ROWS, HD), 1)
    lane = lax.broadcasted_iota(jnp.int32, (1, HD), 1)

    def put_squares(values, which):
        column = jnp.sum(values * values, axis=1, keepdims=True)
        row = jnp.sum(jnp.where(diagonal, column, 0.0), axis=0, keepdims=True)
        ss_send[which] = row
        ss_recv[which, s] = row

    def send_squares(which, d):
        remote(ss_send.at[which], ss_recv.at[which, s], ss_send_sem.at[which], ss_recv_sem.at[which],
               (side, shard_peer(d), t)).start()

    def squares_factor(which):
        wait_bytes(ss_recv.at[which, pl.ds(0, SHARDS - 1)], ss_recv_sem.at[which])
        return lax.rsqrt(jnp.sum(ss_recv[which], axis=0) / D + EPSILON)

    def attention():
        @pl.when(side == 0)
        def _():
            first_loads[0].wait()
            first_loads[1].wait()
            first_loads[2].wait()

        values = x_buf[...].astype(F32)
        put_squares(values, 2)
        mixed = jnp.dot((values * again[...]).astype(BF), wqkv[...], preferred_element_type=F32)
        for part in range(6):
            stage[pl.ds(part, ROWS, stride=8), :] = mixed[:, HD * part:HD * (part + 1)]
        send1[...] = stage[...].astype(BF).reshape(SHARDS, 16, HD)
        recv1[s] = send1[s]

        @pl.when(side == 0)
        def _():
            pl.semaphore_wait(barrier, 2 * SHARDS - 1)

        def go1(d):
            to = shard_peer(d)
            send_squares(2, d)
            remote(send1.at[to], recv1.at[s], send1_sem, recv1_sem, (side, to, t)).start()

        loop(1, SHARDS, go1)

        @pl.when(side == 0)
        def _():
            pushes[0].start()
            first_loads[3].wait()
            first_loads[4].wait()

        lens_here = [lens[2 * s + i] for i in range(2)]
        upper_row = lax.broadcasted_iota(jnp.int32, (16, 1), 0) >= 8
        position = jnp.where(upper_row, lens_here[1], lens_here[0])
        angle = position.astype(F32) * freq[...]
        cosine = jnp.cos(angle)
        sine = jnp.where(lane < HD // 2, -jnp.sin(angle), jnp.sin(angle))

        factor = squares_factor(2)
        scale_ref[0:1, :] = factor[:, :ROWS]
        own_factor = jnp.sum(
            jnp.where(lane == jnp.where(upper_row, 2 * s + 1, 2 * s), factor, 0.0), axis=1, keepdims=True)
        wait_bytes(recv1.at[pl.ds(0, SHARDS - 1)], recv1_sem)
        own = jnp.sum(recv1[...].astype(F32), axis=0) * own_factor
        rotated = own * cosine + pltpu.roll(own, HD // 2, 1) * sine
        rotated = rotated.astype(BF).astype(F32)
        own_values = own.astype(BF).astype(F32)
        new_key = jnp.concatenate(
            [jnp.broadcast_to(rotated[8 * i + 4:8 * i + 5], (8, HD)) for i in range(2)], axis=0)
        new_value = jnp.concatenate(
            [jnp.broadcast_to(own_values[8 * i + 5:8 * i + 6], (8, HD)) for i in range(2)], axis=0)
        own_score = jnp.sum(rotated * new_key, axis=1, keepdims=True) * HD ** (-0.5)
        both = jnp.concatenate(
            [jnp.where(upper_row, 0.0, rotated), jnp.where(upper_row, rotated, 0.0)], axis=1).astype(BF)

        @pl.when(side == 0)
        def _():
            for load in cache_loads:
                load.wait()

        scores = nt_dot(both, kbuf[...]) * HD ** (-0.5)
        at = lax.broadcasted_iota(jnp.int32, (16, CTX), 1)
        scores = jnp.where(at < position, scores, -1e30)
        top = jnp.maximum(jnp.max(scores, axis=1, keepdims=True), own_score)
        weights = jnp.exp(scores - top)
        own_weight = jnp.exp(own_score - top)
        total = jnp.sum(weights, axis=1, keepdims=True) + own_weight
        mixed_values = jnp.dot(weights.astype(BF), vbuf[...], preferred_element_type=F32)
        mixed_values = jnp.concatenate([mixed_values[:8, :HD], mixed_values[8:, HD:]], axis=0)
        mixed_values = mixed_values + own_weight.astype(BF).astype(F32) * new_value
        heads = (mixed_values / total).astype(BF)
        send2[...] = heads

        @pl.when(side == 1)
        def _():
            recv2[1, s] = heads

        @pl.when(side == 0)
        def _():
            remote(send2, recv2.at[side, s], send2_sem, recv2_sem.at[side], mate).start()

        loop(1, SHARDS, lambda d: remote(
            send2, recv2.at[side, s], send2_sem, recv2_sem.at[side], (1, shard_peer(d), t)).start())

    def prepare(slot):
        for load in gu_loads:
            load.wait()
        out_row = lax.broadcasted_iota(jnp.int32, (512, 512), 0)
        in_row = lax.broadcasted_iota(jnp.int32, (512, 512), 1)
        wanted = jnp.where(out_row < 256, 2 * out_row, 2 * (out_row - 256) + 1)
        pick = jnp.where(in_row == wanted, 1.0, 0.0).astype(BF)

        def one(o):
            for half in range(2):
                apart = jnp.dot(pick, graw[2 * o + half].reshape(512, HD), preferred_element_type=F32).astype(BF)
                wgu[slot, o, :, HD * half:HD * (half + 1)] = apart[:256]
                wgu[slot, o, :, 256 + HD * half:256 + HD * (half + 1)] = apart[256:]

        loop(0, OWNERS, one)

    owner = 2 * (s // 4) + s % 4 - 1
    owns = (s % 4 >= 1) & (s % 4 <= 2) & (owner < OWNERS)

    def layer(l):
        @pl.when(l == 0)
        def _():
            wait_bytes(wout.at[0], push_recv.at[0])
            wait_bytes(recv2.at[0], recv2_sem.at[0])

        @pl.when(l == 1)
        def _():
            own_loads[2].wait()
            wait_bytes(recv2.at[1, pl.ds(0, SHARDS - 1)], recv2_sem.at[1])

        heads_f32[...] = recv2[l].astype(F32).reshape(16 * SHARDS, HD)
        gathered = jnp.concatenate(
            [heads_f32[pl.ds(g, ROWS, stride=8), :] for g in range(4)], axis=1).astype(BF)
        projected = jnp.dot(gathered, wout[l], preferred_element_type=F32).astype(BF)
        send3[l] = projected
        recv3[l, t] = projected
        loop(1, TPS, lambda d: remote(
            send3.at[l], recv3.at[l, t], send_sem.at[l, 0], recv_sem.at[l, 0], (1, s, tp_peer(d))).start())

        @pl.when(l == 0)
        def _():
            own_loads[0].wait()

        @pl.when(l == 1)
        def _():
            wait_bytes(fgain.at[1], push_recv.at[1])
            wait_bytes(wgu.at[1], push_recv.at[3])

        wait_bytes(recv3.at[l, pl.ds(0, TPS - 1)], recv_sem.at[l, 0])
        after = (x_buf[...].astype(F32) + jnp.sum(recv3[l].astype(F32), axis=0)).astype(BF)
        a_buf[...] = after
        values = after.astype(F32)
        put_squares(values, l)
        loop(1, SHARDS, lambda d: send_squares(l, d))
        scaled = (values * fgain[l]).astype(BF)

        def go4(d):
            o = lax.rem(s + d, OWNERS)
            to = 4 * (o // 2) + 1 + o % 2
            both = jnp.dot(scaled, wgu[l, o], preferred_element_type=F32).astype(BF)

            @pl.when(to == s)
            def _():
                recv4[l, s] = both

            @pl.when(to != s)
            def _():
                send4[l, o] = both
                remote(send4.at[l, o], recv4.at[l, s], send_sem.at[l, 1], recv_sem.at[l, 1], (1, to, t)).start()

        loop(0, OWNERS, go4)
        factor = squares_factor(l)
        column = jnp.sum(jnp.where(diagonal, factor, 0.0), axis=1, keepdims=True)

        @pl.when(owns)
        def _():
            wait_bytes(recv4.at[l, pl.ds(0, SHARDS - 1)], recv_sem.at[l, 1])
            both = jnp.sum(recv4[l].astype(F32), axis=0) * column
            gate, up = both[:, :256], both[:, 256:]
            hidden = (gate / (1.0 + jnp.exp(-gate)) * up).astype(BF)
            send5[l] = hidden
            recv5[l, owner] = hidden
            loop(1, SHARDS, lambda d: remote(
                send5.at[l], recv5.at[l, owner], send_sem.at[l, 2], recv_sem.at[l, 2],
                (1, shard_peer(d), t)).start())

        @pl.when(l == 0)
        def _():
            scale_ref[1:2, :] = factor[:, :ROWS]
            own_loads[1].wait()

        @pl.when(l == 1)
        def _():
            end_scale[...] = factor
            remote(end_scale, end_scale, end_send.at[1], end_recv.at[1], mate).start()
            wait_bytes(wdn.at[1], push_recv.at[2])

        @pl.when(owns)
        def _():
            wait_bytes(recv5.at[l, pl.ds(0, OWNERS - 1)], recv_sem.at[l, 2])

        @pl.when(jnp.logical_not(owns))
        def _():
            wait_bytes(recv5.at[l], recv_sem.at[l, 2])

        hidden_all = jnp.concatenate([recv5[l, o] for o in range(OWNERS)], axis=1)
        partial = jnp.dot(hidden_all, wdn[l], preferred_element_type=F32).astype(BF)
        send6[l] = partial
        recv6[l, t] = partial
        loop(1, TPS, lambda d: remote(
            send6.at[l], recv6.at[l, t], send_sem.at[l, 3], recv_sem.at[l, 3], (1, s, tp_peer(d))).start())
        wait_bytes(recv6.at[l, pl.ds(0, TPS - 1)], recv_sem.at[l, 3])
        result = (a_buf[...].astype(F32) + jnp.sum(recv6[l].astype(F32), axis=0)).astype(BF)

        @pl.when(l == 0)
        def _():
            x_buf[...] = result
            out_ref[...] = result

        @pl.when(l == 1)
        def _():
            end_buf[...] = result
            remote(end_buf, end_buf, end_send.at[0], end_recv.at[0], mate).start()

    @pl.when(side == 1)
    def _():
        prepare(0)
        for load in first_loads + cache_loads:
            load.wait()
        pl.semaphore_wait(barrier, SHARDS - 1 + TPS - 1 + 1)

    def step(l):
        pl.when(side == l)(attention)

        @pl.when(side == 1)
        def _():
            layer(l)

    loop(0, 2, step)

    wait_bytes(ss_recv.at[2, pl.ds(0, SHARDS - 1)], ss_send_sem.at[2])
    wait_bytes(recv1.at[pl.ds(0, SHARDS - 1)], send1_sem)

    @pl.when(side == 0)
    def _():
        prepare(1)
        for push in pushes[1:]:
            push.start()
        wait_bytes(recv2.at[0], send2_sem)
        for push in pushes:
            push.wait_send()
        wait_bytes(end_scale, end_recv.at[1])
        scale_ref[1:2, :] = end_scale[:, :ROWS]
        wait_bytes(end_buf, end_recv.at[0])
        out_ref[...] = end_buf[...]

    @pl.when(side == 1)
    def _():
        wait_bytes(recv2.at[1, pl.ds(0, SHARDS - 1)], send2_sem)

        def sent(l):
            wait_bytes(ss_recv.at[l, pl.ds(0, SHARDS - 1)], ss_send_sem.at[l])
            wait_bytes(recv3.at[l, pl.ds(0, TPS - 1)], send_sem.at[l, 0])
            wait_bytes(recv6.at[l, pl.ds(0, TPS - 1)], send_sem.at[l, 3])

            @pl.when(owns)
            def _():
                wait_bytes(recv4.at[l, pl.ds(0, OWNERS - 1)], send_sem.at[l, 1])
                wait_bytes(recv4.at[l, pl.ds(0, SHARDS - 1), :, pl.ds(0, 256)], send_sem.at[l, 2])

            @pl.when(jnp.logical_not(owns))
            def _():
                wait_bytes(recv4.at[l, pl.ds(0, OWNERS)], send_sem.at[l, 1])

        loop(0, 2, sent)
        wait_bytes(end_buf, end_send.at[0])
        wait_bytes(end_scale, end_send.at[1])


def body(tokens, lengths, kv_cache, attn_gain, qkv_weight, out_weight, ffn_gain, gate_up, down_weight):
    freqs = (ROPE_BASE ** (-np.arange(HD // 2, dtype=np.float64) * 2.0 / HD)).astype(np.float32)
    freqs = jnp.asarray(np.concatenate([freqs, freqs])[None])
    vmem = pl.BlockSpec(memory_space=pltpu.VMEM)
    hbm = pl.BlockSpec(memory_space=pltpu.HBM)
    dma = pltpu.SemaphoreType.DMA
    out, scales = pl.pallas_call(
        kernel,
        out_shape=(jax.ShapeDtypeStruct((ROWS, 256), BF), jax.ShapeDtypeStruct((2, ROWS), F32)),
        in_specs=[hbm] * 10,
        out_specs=(vmem, vmem),
        scratch_shapes=[
            pltpu.SMEM((ROWS,), jnp.int32),
            pltpu.VMEM((1, 256), F32), pltpu.VMEM((2, 1, 256), F32), pltpu.VMEM((1, HD), F32),
            pltpu.VMEM((CTX, 2 * HD), BF), pltpu.VMEM((CTX, 2 * HD), BF),
            pltpu.VMEM((256, 768), BF), pltpu.VMEM((2, 512, 256), BF),
            pltpu.VMEM((TILES, 256, 2, HD), BF), pltpu.VMEM((2, OWNERS, 256, 512), BF),
            pltpu.VMEM((2, TILES * HD, 256), BF),
            pltpu.VMEM((ROWS, 256), BF), pltpu.VMEM((ROWS, 256), BF),
            pltpu.VMEM((3, 1, HD), F32), pltpu.VMEM((3, SHARDS, 1, HD), F32),
            pltpu.VMEM((16 * SHARDS, HD), F32), pltpu.VMEM((SHARDS, 16, HD), BF), pltpu.VMEM((SHARDS, 16, HD), BF),
            pltpu.VMEM((16, HD), BF), pltpu.VMEM((2, SHARDS, 16, HD), BF), pltpu.VMEM((16 * SHARDS, HD), F32),
            pltpu.VMEM((2, ROWS, 256), BF), pltpu.VMEM((2, TPS, ROWS, 256), BF),
            pltpu.VMEM((2, OWNERS, ROWS, 512), BF), pltpu.VMEM((2, SHARDS, ROWS, 512), BF),
            pltpu.VMEM((2, ROWS, 256), BF), pltpu.VMEM((2, OWNERS, ROWS, 256), BF),
            pltpu.VMEM((2, ROWS, 256), BF), pltpu.VMEM((2, TPS, ROWS, 256), BF),
            pltpu.VMEM((ROWS, 256), BF), pltpu.VMEM((1, HD), F32),
            dma((12,)), dma((TILES,)), dma((3,)), dma((3,)), dma, dma, dma, dma((2,)),
            dma((2, 4)), dma((2, 4)), dma((4,)), dma((4,)), dma((2,)), dma((2,)),
        ],
        compiler_params=pltpu.CompilerParams(
            collective_id=0, has_side_effects=True, vmem_limit_bytes=63 * 1024 * 1024),
        cost_estimate=pl.CostEstimate(flops=130_000_000, bytes_accessed=7_500_000, transcendentals=70_000),
    )(
        tokens, lengths, attn_gain, ffn_gain, freqs,
        kv_cache.reshape(2, CTX, 2 * HD), qkv_weight.reshape(256, 768), out_weight.reshape(512, 256),
        gate_up.reshape(256, 2, 1792), down_weight.reshape(1792, 256),
    )
    return (out[None], scales[None])


def solution(mesh):
    in_specs = (
        P(None, "shard"),
        P(),
        P("side", "shard", None, "tp", None),
        P("side", "shard"),
        P("side", "shard", "tp", None),
        P("side", "tp", None, "shard"),
        P("side", "shard"),
        P("side", "shard", None, "tp"),
        P("side", "tp", "shard"),
    )
    out_specs = (P("side", None, "shard"), P("side", None, None))
    return jax.shard_map(body, mesh=mesh, in_specs=in_specs, out_specs=out_specs, check_vma=False)
```

```python
import functools

import jax
import jax.numpy as jnp
import numpy as np
from jax import lax
from jax.experimental import pallas as pl
from jax.experimental.pallas import tpu as pltpu
from jax.sharding import PartitionSpec as P

D = 4096
HD = 128
ROWS = 32
EPSILON = 1e-05
ROPE_BASE = 500000.0
SHARDS = 16
TPS = 8
TILES = 14
OWNERS = 7
CTX = 4096
CHUNK = 1024
BF = jnp.bfloat16
F32 = jnp.float32
MESH = pl.DeviceIdType.MESH


def nt_dot(a, b):
    return lax.dot_general(a, b, (((1,), (1,)), ((), ())), preferred_element_type=F32)


def wait_bytes(ref, sem):
    pltpu.make_async_copy(ref, ref, sem).wait()


def remote(src, dst, ssem, rsem, device):
    return pltpu.make_async_remote_copy(
        src_ref=src, dst_ref=dst, send_sem=ssem, recv_sem=rsem, device_id=device, device_id_type=MESH)


def kernel(
    tok_hbm, lens_hbm, again_hbm, fgain_hbm, freq_hbm, cache_hbm, wqkv_hbm, wout_hbm, wgu_hbm, wdn_hbm,
    out_ref, scale_ref,
    lens, again, fgain, freq,
    kbuf, vbuf, keys_t, wqkv, wout, graw, wgu, wdn,
    x_buf, a_buf,
    ss_send, ss_recv, stage, send1, recv1, send2, recv2, heads_f32,
    send3, recv3, send4, recv4, send5, recv5, send6, recv6, end_scale,
    load_sem, gu_sem, ss_send_sem, ss_recv_sem, send1_sem, recv1_sem, send2_sem, recv2_sem,
    send_sem, recv_sem, recv6_sem, push_send, push_recv, end_send, end_recv,
):
    side = lax.axis_index("side")
    s = lax.axis_index("shard")
    t = lax.axis_index("tp")
    mate = (1 - side, s, t)

    def shard_peer(d):
        return lax.rem(s + d, SHARDS)

    def tp_peer(d):
        return lax.rem(t + d, TPS)

    barrier = pltpu.get_barrier_semaphore()

    def greet(device):
        pl.semaphore_signal(barrier, inc=1, device_id=device, device_id_type=MESH)

    def loop(start, stop, step):
        def go(d, carry):
            step(d)
            return carry

        lax.fori_loop(start, stop, go, 0)

    @pl.when(side == 0)
    def _():
        loop(1, SHARDS, lambda d: greet((0, shard_peer(d), t)))
        loop(0, TPS, lambda d: greet((1, s, tp_peer(d))))

    @pl.when(side == 1)
    def _():
        loop(0, SHARDS, lambda d: greet((0, shard_peer(d), t)))
        loop(1, SHARDS, lambda d: greet((1, shard_peer(d), t)))
        loop(1, TPS, lambda d: greet((1, s, tp_peer(d))))

    first_loads = [
        pltpu.make_async_copy(tok_hbm, x_buf, load_sem.at[0]),
        pltpu.make_async_copy(again_hbm, again, load_sem.at[1]),
        pltpu.make_async_copy(wqkv_hbm, wqkv, load_sem.at[2]),
        pltpu.make_async_copy(lens_hbm, lens, load_sem.at[3]),
        pltpu.make_async_copy(freq_hbm, freq, load_sem.at[4]),
    ]
    cache_loads = []
    for i in range(2):
        cache_loads.append(pltpu.make_async_copy(
            cache_hbm.at[i, :, pl.ds(0, HD)], kbuf.at[:, pl.ds(HD * i, HD)], load_sem.at[5 + i]))
        cache_loads.append(pltpu.make_async_copy(
            cache_hbm.at[i, :, pl.ds(HD, HD)], vbuf.at[:, pl.ds(HD * i, HD)], load_sem.at[7 + i]))
    own_loads = [
        pltpu.make_async_copy(fgain_hbm, fgain.at[0], load_sem.at[9]),
        pltpu.make_async_copy(wdn_hbm, wdn.at[0], load_sem.at[10]),
        pltpu.make_async_copy(wout_hbm, wout.at[1], load_sem.at[11]),
    ]
    gu_loads = [
        pltpu.make_async_copy(wgu_hbm.at[:, :, pl.ds(HD * j, HD)], graw.at[j], gu_sem.at[j]) for j in range(TILES)
    ]
    for load in first_loads:
        load.start()

    @pl.when(side == 0)
    def _():
        for load in cache_loads:
            load.start()

    for load in gu_loads:
        load.start()

    @pl.when(side == 1)
    def _():
        for load in own_loads:
            load.start()
        for load in cache_loads:
            load.start()

    pushes = [
        remote(wout_hbm, wout.at[0], push_send.at[0], push_recv.at[0], mate),
        remote(fgain_hbm, fgain.at[1], push_send.at[1], push_recv.at[1], mate),
        remote(wdn_hbm, wdn.at[1], push_send.at[2], push_recv.at[2], mate),
        remote(wgu.at[1], wgu.at[1], push_send.at[3], push_recv.at[3], mate),
    ]

    stage[...] = jnp.zeros_like(stage)
    diagonal = lax.broadcasted_iota(jnp.int32, (ROWS, HD), 0) == lax.broadcasted_iota(jnp.int32, (ROWS, HD), 1)
    lane = lax.broadcasted_iota(jnp.int32, (1, HD), 1)

    def put_squares(values, which):
        column = jnp.sum(values * values, axis=1, keepdims=True)
        row = jnp.sum(jnp.where(diagonal, column, 0.0), axis=0, keepdims=True)
        ss_send[which] = row
        ss_recv[which, s] = row

    def send_squares(which, d):
        remote(ss_send.at[which], ss_recv.at[which, s], ss_send_sem.at[which], ss_recv_sem.at[which],
               (side, shard_peer(d), t)).start()

    def squares_factor(which):
        wait_bytes(ss_recv.at[which, pl.ds(0, SHARDS - 1)], ss_recv_sem.at[which])
        return lax.rsqrt(jnp.sum(ss_recv[which], axis=0) / D + EPSILON)

    def turn_keys():
        for load in cache_loads:
            load.wait()
        eye = jnp.where(
            lax.broadcasted_iota(jnp.int32, (256, 256), 0) == lax.broadcasted_iota(jnp.int32, (256, 256), 1),
            1.0, 0.0).astype(BF)

        def turn(c):
            at = pl.ds(pl.multiple_of(512 * c, 512), 512)
            keys_t[:, at] = nt_dot(eye, kbuf[at, :]).astype(BF)

        loop(0, CTX // 512, turn)

    def attention():
        @pl.when(side == 0)
        def _():
            first_loads[0].wait()
            first_loads[1].wait()
            first_loads[2].wait()

        values = x_buf[...].astype(F32)
        put_squares(values, 2)
        mixed = jnp.dot((values * again[...]).astype(BF), wqkv[...], preferred_element_type=F32)
        for part in range(6):
            stage[pl.ds(part, ROWS, stride=8), :] = mixed[:, HD * part:HD * (part + 1)]
        send1[...] = stage[...].astype(BF).reshape(SHARDS, 16, HD)
        recv1[s] = send1[s]

        @pl.when(side == 0)
        def _():
            pl.semaphore_wait(barrier, 2 * SHARDS - 1)

        def go1(d):
            to = shard_peer(d)
            send_squares(2, d)
            remote(send1.at[to], recv1.at[s], send1_sem, recv1_sem, (side, to, t)).start()

        loop(1, SHARDS, go1)

        @pl.when(side == 0)
        def _():
            pushes[0].start()
            first_loads[3].wait()
            first_loads[4].wait()
            turn_keys()

        lens_here = [lens[2 * s + i] for i in range(2)]
        upper_row = lax.broadcasted_iota(jnp.int32, (16, 1), 0) >= 8
        position = jnp.where(upper_row, lens_here[1], lens_here[0])
        angle = position.astype(F32) * freq[...]
        cosine = jnp.cos(angle)
        sine = jnp.where(lane < HD // 2, -jnp.sin(angle), jnp.sin(angle))

        factor = squares_factor(2)
        scale_ref[0:1, :] = factor[:, :ROWS]
        own_factor = jnp.sum(
            jnp.where(lane == jnp.where(upper_row, 2 * s + 1, 2 * s), factor, 0.0), axis=1, keepdims=True)
        wait_bytes(recv1.at[pl.ds(0, SHARDS - 1)], recv1_sem)
        own = jnp.sum(recv1[...].astype(F32), axis=0) * own_factor
        rotated = own * cosine + pltpu.roll(own, HD // 2, 1) * sine
        rotated = rotated.astype(BF).astype(F32)
        own_values = own.astype(BF).astype(F32)
        new_key = jnp.concatenate(
            [jnp.broadcast_to(rotated[8 * i + 4:8 * i + 5], (8, HD)) for i in range(2)], axis=0)
        new_value = jnp.concatenate(
            [jnp.broadcast_to(own_values[8 * i + 5:8 * i + 6], (8, HD)) for i in range(2)], axis=0)
        own_score = jnp.sum(rotated * new_key, axis=1, keepdims=True) * HD ** (-0.5)
        both = jnp.concatenate(
            [jnp.where(upper_row, 0.0, rotated), jnp.where(upper_row, rotated, 0.0)], axis=1).astype(BF)

        tops, sums, parts = [], [], []
        for c in range(CTX // CHUNK):
            scores = jnp.dot(both, keys_t[:, CHUNK * c:CHUNK * (c + 1)], preferred_element_type=F32) * HD ** (-0.5)
            at = lax.broadcasted_iota(jnp.int32, (16, CHUNK), 1) + CHUNK * c
            scores = jnp.where(at < position, scores, -1e30)
            chunk_top = jnp.maximum(jnp.max(scores, axis=1, keepdims=True), own_score)
            weights = jnp.exp(scores - chunk_top)
            tops.append(chunk_top)
            sums.append(jnp.sum(weights, axis=1, keepdims=True))
            parts.append(jnp.dot(
                weights.astype(BF), vbuf[CHUNK * c:CHUNK * (c + 1), :], preferred_element_type=F32))
        top = functools.reduce(jnp.maximum, tops)
        own_weight = jnp.exp(own_score - top)
        total, mixed_values = own_weight, 0.0
        for chunk_top, chunk_sum, part in zip(tops, sums, parts):
            share = jnp.exp(chunk_top - top)
            total = total + share * chunk_sum
            mixed_values = mixed_values + share * part
        mixed_values = jnp.concatenate([mixed_values[:8, :HD], mixed_values[8:, HD:]], axis=0)
        mixed_values = mixed_values + own_weight.astype(BF).astype(F32) * new_value
        heads = (mixed_values / total).astype(BF)
        send2[...] = heads

        @pl.when(side == 1)
        def _():
            recv2[1, s] = heads

        @pl.when(side == 0)
        def _():
            remote(send2, recv2.at[side, s], send2_sem, recv2_sem.at[side], mate).start()

        loop(1, SHARDS, lambda d: remote(
            send2, recv2.at[side, s], send2_sem, recv2_sem.at[side], (1, shard_peer(d), t)).start())

    def prepare(slot):
        for load in gu_loads:
            load.wait()
        out_row = lax.broadcasted_iota(jnp.int32, (512, 512), 0)
        in_row = lax.broadcasted_iota(jnp.int32, (512, 512), 1)
        wanted = jnp.where(out_row < 256, 2 * out_row, 2 * (out_row - 256) + 1)
        pick = jnp.where(in_row == wanted, 1.0, 0.0).astype(BF)

        def one(o):
            for half in range(2):
                apart = jnp.dot(pick, graw[2 * o + half].reshape(512, HD), preferred_element_type=F32).astype(BF)
                wgu[slot, o, :, HD * half:HD * (half + 1)] = apart[:256]
                wgu[slot, o, :, 256 + HD * half:256 + HD * (half + 1)] = apart[256:]

        loop(0, OWNERS, one)

    owner = 2 * (s // 4) + s % 4 - 1
    owns = (s % 4 >= 1) & (s % 4 <= 2) & (owner < OWNERS)

    def layer(l):
        @pl.when(l == 0)
        def _():
            wait_bytes(wout.at[0], push_recv.at[0])
            wait_bytes(recv2.at[0], recv2_sem.at[0])

        @pl.when(l == 1)
        def _():
            own_loads[2].wait()
            wait_bytes(recv2.at[1, pl.ds(0, SHARDS - 1)], recv2_sem.at[1])

        heads_f32[...] = recv2[l].astype(F32).reshape(16 * SHARDS, HD)
        gathered = jnp.concatenate(
            [heads_f32[pl.ds(g, ROWS, stride=8), :] for g in range(4)], axis=1).astype(BF)
        projected = jnp.dot(gathered, wout[l], preferred_element_type=F32).astype(BF)
        send3[l] = projected
        recv3[l, t] = projected
        loop(1, TPS, lambda d: remote(
            send3.at[l], recv3.at[l, t], send_sem.at[l, 0], recv_sem.at[l, 0], (1, s, tp_peer(d))).start())

        @pl.when(l == 0)
        def _():
            own_loads[0].wait()

        @pl.when(l == 1)
        def _():
            wait_bytes(fgain.at[1], push_recv.at[1])
            wait_bytes(wgu.at[1], push_recv.at[3])

        wait_bytes(recv3.at[l, pl.ds(0, TPS - 1)], recv_sem.at[l, 0])
        after = (x_buf[...].astype(F32) + jnp.sum(recv3[l].astype(F32), axis=0)).astype(BF)
        a_buf[...] = after
        values = after.astype(F32)
        put_squares(values, l)
        loop(1, SHARDS, lambda d: send_squares(l, d))
        scaled = (values * fgain[l]).astype(BF)

        for o in range(OWNERS):
            send4[l, o] = jnp.dot(scaled, wgu[l, o], preferred_element_type=F32).astype(BF)

        @pl.when(owns)
        def _():
            recv4[l, s] = send4[l, jnp.where(owns, owner, 0)]

        def go4(d):
            o = lax.rem(s + d, OWNERS)
            to = 4 * (o // 2) + 1 + o % 2

            @pl.when(to != s)
            def _():
                remote(send4.at[l, o], recv4.at[l, s], send_sem.at[l, 1], recv_sem.at[l, 1], (1, to, t)).start()

        loop(0, OWNERS, go4)
        factor = squares_factor(l)
        column = jnp.sum(jnp.where(diagonal, factor, 0.0), axis=1, keepdims=True)

        @pl.when(owns)
        def _():
            wait_bytes(recv4.at[l, pl.ds(0, SHARDS - 1)], recv_sem.at[l, 1])
            both = jnp.sum(recv4[l].astype(F32), axis=0) * column
            gate, up = both[:, :256], both[:, 256:]
            hidden = (gate / (1.0 + jnp.exp(-gate)) * up).astype(BF)
            send5[l] = hidden
            recv5[l, owner] = hidden
            loop(1, SHARDS, lambda d: remote(
                send5.at[l], recv5.at[l, owner], send_sem.at[l, 2], recv_sem.at[l, 2],
                (1, shard_peer(d), t)).start())

        @pl.when(l == 0)
        def _():
            scale_ref[1:2, :] = factor[:, :ROWS]
            own_loads[1].wait()

        @pl.when(l == 1)
        def _():
            end_scale[...] = factor
            remote(end_scale, end_scale, end_send.at[1], end_recv.at[1], mate).start()
            remote(a_buf, a_buf, end_send.at[0], end_recv.at[0], mate).start()
            wait_bytes(wdn.at[1], push_recv.at[2])

        @pl.when(owns)
        def _():
            wait_bytes(recv5.at[l, pl.ds(0, OWNERS - 1)], recv_sem.at[l, 2])

        @pl.when(jnp.logical_not(owns))
        def _():
            wait_bytes(recv5.at[l], recv_sem.at[l, 2])

        hidden_all = jnp.concatenate([recv5[l, o] for o in range(OWNERS)], axis=1)
        partial = jnp.dot(hidden_all, wdn[l], preferred_element_type=F32).astype(BF)
        send6[l] = partial

        @pl.when(l == 0)
        def _():
            recv6[t] = partial
            loop(1, TPS, lambda d: remote(
                send6.at[l], recv6.at[t], send_sem.at[l, 3], recv6_sem, (1, s, tp_peer(d))).start())
            wait_bytes(recv6.at[pl.ds(0, TPS - 1)], recv6_sem)
            result = (a_buf[...].astype(F32) + jnp.sum(recv6[...].astype(F32), axis=0)).astype(BF)
            x_buf[...] = result
            out_ref[...] = result

        @pl.when(l == 1)
        def _():
            loop(0, TPS, lambda d: remote(
                send6.at[l], recv6.at[t], send_sem.at[l, 3], recv6_sem, (0, s, tp_peer(d))).start())

    @pl.when(side == 1)
    def _():
        prepare(0)
        for load in first_loads:
            load.wait()
        turn_keys()
        pl.semaphore_wait(barrier, SHARDS - 1 + TPS - 1 + TPS)

    def step(l):
        pl.when(side == l)(attention)

        @pl.when(side == 1)
        def _():
            layer(l)

    loop(0, 2, step)

    wait_bytes(ss_recv.at[2, pl.ds(0, SHARDS - 1)], ss_send_sem.at[2])
    wait_bytes(recv1.at[pl.ds(0, SHARDS - 1)], send1_sem)

    @pl.when(side == 0)
    def _():
        prepare(1)
        for push in pushes[1:]:
            push.start()
        wait_bytes(recv2.at[0], send2_sem)
        for push in pushes:
            push.wait_send()
        wait_bytes(end_scale, end_recv.at[1])
        scale_ref[1:2, :] = end_scale[:, :ROWS]
        wait_bytes(a_buf, end_recv.at[0])
        wait_bytes(recv6, recv6_sem)
        out_ref[...] = (a_buf[...].astype(F32) + jnp.sum(recv6[...].astype(F32), axis=0)).astype(BF)

    @pl.when(side == 1)
    def _():
        wait_bytes(recv2.at[1, pl.ds(0, SHARDS - 1)], send2_sem)

        def sent(l):
            wait_bytes(ss_recv.at[l, pl.ds(0, SHARDS - 1)], ss_send_sem.at[l])
            wait_bytes(recv3.at[l, pl.ds(0, TPS - 1)], send_sem.at[l, 0])

            @pl.when(owns)
            def _():
                wait_bytes(recv4.at[l, pl.ds(0, OWNERS - 1)], send_sem.at[l, 1])
                wait_bytes(recv4.at[l, pl.ds(0, SHARDS - 1), :, pl.ds(0, 256)], send_sem.at[l, 2])

            @pl.when(jnp.logical_not(owns))
            def _():
                wait_bytes(recv4.at[l, pl.ds(0, OWNERS)], send_sem.at[l, 1])

        loop(0, 2, sent)
        wait_bytes(recv6.at[pl.ds(0, TPS - 1)], send_sem.at[0, 3])
        wait_bytes(recv6, send_sem.at[1, 3])
        wait_bytes(a_buf, end_send.at[0])
        wait_bytes(end_scale, end_send.at[1])


def body(tokens, lengths, kv_cache, attn_gain, qkv_weight, out_weight, ffn_gain, gate_up, down_weight):
    freqs = (ROPE_BASE ** (-np.arange(HD // 2, dtype=np.float64) * 2.0 / HD)).astype(np.float32)
    freqs = jnp.asarray(np.concatenate([freqs, freqs])[None])
    vmem = pl.BlockSpec(memory_space=pltpu.VMEM)
    hbm = pl.BlockSpec(memory_space=pltpu.HBM)
    dma = pltpu.SemaphoreType.DMA
    out, scales = pl.pallas_call(
        kernel,
        out_shape=(pltpu.VMEM((ROWS, 256), BF), pltpu.VMEM((2, ROWS), F32)),
        in_specs=[hbm] * 10,
        out_specs=(vmem, vmem),
        scratch_shapes=[
            pltpu.SMEM((ROWS,), jnp.int32),
            pltpu.VMEM((1, 256), F32), pltpu.VMEM((2, 1, 256), F32), pltpu.VMEM((1, HD), F32),
            pltpu.VMEM((CTX, 2 * HD), BF), pltpu.VMEM((CTX, 2 * HD), BF), pltpu.VMEM((2 * HD, CTX), BF),
            pltpu.VMEM((256, 768), BF), pltpu.VMEM((2, 512, 256), BF),
            pltpu.VMEM((TILES, 256, 2, HD), BF), pltpu.VMEM((2, OWNERS, 256, 512), BF),
            pltpu.VMEM((2, TILES * HD, 256), BF),
            pltpu.VMEM((ROWS, 256), BF), pltpu.VMEM((ROWS, 256), BF),
            pltpu.VMEM((3, 1, HD), F32), pltpu.VMEM((3, SHARDS, 1, HD), F32),
            pltpu.VMEM((16 * SHARDS, HD), F32), pltpu.VMEM((SHARDS, 16, HD), BF), pltpu.VMEM((SHARDS, 16, HD), BF),
            pltpu.VMEM((16, HD), BF), pltpu.VMEM((2, SHARDS, 16, HD), BF), pltpu.VMEM((16 * SHARDS, HD), F32),
            pltpu.VMEM((2, ROWS, 256), BF), pltpu.VMEM((2, TPS, ROWS, 256), BF),
            pltpu.VMEM((2, OWNERS, ROWS, 512), BF), pltpu.VMEM((2, SHARDS, ROWS, 512), BF),
            pltpu.VMEM((2, ROWS, 256), BF), pltpu.VMEM((2, OWNERS, ROWS, 256), BF),
            pltpu.VMEM((2, ROWS, 256), BF), pltpu.VMEM((TPS, ROWS, 256), BF),
            pltpu.VMEM((1, HD), F32),
            dma((12,)), dma((TILES,)), dma((3,)), dma((3,)), dma, dma, dma, dma((2,)),
            dma((2, 4)), dma((2, 3)), dma, dma((4,)), dma((4,)), dma((2,)), dma((2,)),
        ],
        compiler_params=pltpu.CompilerParams(
            collective_id=0, has_side_effects=True, vmem_limit_bytes=63 * 1024 * 1024),
        cost_estimate=pl.CostEstimate(flops=130_000_000, bytes_accessed=7_500_000, transcendentals=70_000),
    )(*(pltpu.with_memory_space_constraint(x, pltpu.HBM) for x in (
        tokens, lengths, attn_gain, ffn_gain, freqs,
        kv_cache.reshape(2, CTX, 2 * HD), qkv_weight.reshape(256, 768), out_weight.reshape(512, 256),
        gate_up.reshape(256, 2, 1792), down_weight.reshape(1792, 256),
    )))
    return (out[None], scales[None])


def solution(mesh):
    in_specs = (
        P(None, "shard"),
        P(),
        P("side", "shard", None, "tp", None),
        P("side", "shard"),
        P("side", "shard", "tp", None),
        P("side", "tp", None, "shard"),
        P("side", "shard"),
        P("side", "shard", None, "tp"),
        P("side", "tp", "shard"),
    )
    out_specs = (P("side", None, "shard"), P("side", None, None))
    return jax.shard_map(body, mesh=mesh, in_specs=in_specs, out_specs=out_specs, check_vma=False)
```

```python
import functools

import jax
import jax.numpy as jnp
import numpy as np
from jax import lax
from jax.experimental import pallas as pl
from jax.experimental.pallas import tpu as pltpu
from jax.sharding import PartitionSpec as P

D = 4096
HD = 128
ROWS = 32
EPSILON = 1e-05
ROPE_BASE = 500000.0
SHARDS = 16
TPS = 8
TILES = 14
OWNERS = 7
CTX = 4096
CHUNK = 1024
BF = jnp.bfloat16
F32 = jnp.float32
MESH = pl.DeviceIdType.MESH


def nt_dot(a, b):
    return lax.dot_general(a, b, (((1,), (1,)), ((), ())), preferred_element_type=F32)


def wait_bytes(ref, sem):
    pltpu.make_async_copy(ref, ref, sem).wait()


def remote(src, dst, ssem, rsem, device):
    return pltpu.make_async_remote_copy(
        src_ref=src, dst_ref=dst, send_sem=ssem, recv_sem=rsem, device_id=device, device_id_type=MESH)


def kernel(
    tok_hbm, lens_hbm, again_hbm, fgain_hbm, freq_hbm, cache_hbm, wqkv_hbm, wout_hbm, wgu_hbm, wdn_hbm,
    out_ref, scale_ref,
    lens, again, fgain, freq,
    kbuf, vbuf, keys_t, wqkv, wout, graw, wgu, wdn,
    x_buf, a_buf,
    ss_send, ss_recv, stage, send1, recv1, send2, recv2, heads_f32,
    send3, recv3, send4, recv4, send5, recv5, send6, recv6, end_scale,
    load_sem, gu_sem, ss_send_sem, ss_recv_sem, send1_sem, recv1_sem, send2_sem, recv2_sem,
    send_sem, recv_sem, recv6_sem, push_send, push_recv, end_send, end_recv, ready,
):
    side = lax.axis_index("side")
    s = lax.axis_index("shard")
    t = lax.axis_index("tp")
    mate = (1 - side, s, t)
    y, x, half = s // 4, t % 4, t // 4
    z = 4 * half + s % 4
    across = (1, s, 4 * (1 - half) + x)

    def shard_peer(d):
        return lax.rem(s + d, SHARDS)

    def tp_peer(d):
        return lax.rem(t + d, TPS)

    def x_peer(d):
        return 4 * half + lax.rem(x + d, 4)

    def plane_peer(at_side, dy, dz):
        to_z = lax.rem(z + dz, 8)
        return (at_side, 4 * lax.rem(y + dy, 4) + lax.rem(to_z, 4), 4 * (to_z // 4) + x)

    barrier = pltpu.get_barrier_semaphore()

    def greet(device):
        pl.semaphore_signal(barrier, inc=1, device_id=device, device_id_type=MESH)

    def loop(start, stop, step):
        def go(d, carry):
            step(d)
            return carry

        lax.fori_loop(start, stop, go, 0)

    def plane(step):
        loop(0, 32, lambda e: step(lax.rem(e // 8 + 2, 4), lax.rem(e + 4, 8)))

    def shard_peers(step):
        loop(8, SHARDS, step)
        loop(1, 8, step)

    def greet_side_1():
        def in_plane(dy, dz):
            @pl.when((side == 0) | (dy != 0) | (dz != 0))
            def _():
                greet(plane_peer(1, dy, dz))

        plane(in_plane)

        def other_x(d):
            greet((1, s, x_peer(d)))
            greet((1, s, lax.rem(4 + x_peer(d), TPS)))

        loop(1, 4, other_x)

    @pl.when(side == 0)
    def _():
        shard_peers(lambda d: greet((0, shard_peer(d), t)))

    greet_side_1()

    first_loads = [
        pltpu.make_async_copy(tok_hbm, x_buf, load_sem.at[0]),
        pltpu.make_async_copy(again_hbm, again, load_sem.at[1]),
        pltpu.make_async_copy(wqkv_hbm, wqkv, load_sem.at[2]),
        pltpu.make_async_copy(lens_hbm, lens, load_sem.at[3]),
        pltpu.make_async_copy(freq_hbm, freq, load_sem.at[4]),
    ]
    cache_loads = []
    for i in range(2):
        cache_loads.append(pltpu.make_async_copy(
            cache_hbm.at[i, :, pl.ds(0, HD)], kbuf.at[:, pl.ds(HD * i, HD)], load_sem.at[5 + i]))
        cache_loads.append(pltpu.make_async_copy(
            cache_hbm.at[i, :, pl.ds(HD, HD)], vbuf.at[:, pl.ds(HD * i, HD)], load_sem.at[7 + i]))
    own_loads = [
        pltpu.make_async_copy(fgain_hbm, fgain.at[0], load_sem.at[9]),
        pltpu.make_async_copy(wdn_hbm, wdn.at[0], load_sem.at[10]),
        pltpu.make_async_copy(wout_hbm, wout.at[1, half], load_sem.at[11]),
    ]
    gu_loads = [
        pltpu.make_async_copy(wgu_hbm.at[:, :, pl.ds(HD * j, HD)], graw.at[j], gu_sem.at[j]) for j in range(TILES)
    ]
    for load in first_loads:
        load.start()

    @pl.when(side == 0)
    def _():
        for load in cache_loads:
            load.start()

    for load in gu_loads:
        load.start()

    @pl.when(side == 1)
    def _():
        for load in own_loads:
            load.start()
        for load in cache_loads:
            load.start()

    pushes = [
        remote(wout_hbm, wout.at[0, half], push_send.at[0], push_recv.at[0], mate),
        remote(wout_hbm, wout.at[0, half], push_send.at[4], push_recv.at[4], across),
        remote(fgain_hbm, fgain.at[1], push_send.at[1], push_recv.at[1], mate),
        remote(wdn_hbm, wdn.at[1], push_send.at[2], push_recv.at[2], mate),
        remote(wgu.at[1], wgu.at[1], push_send.at[3], push_recv.at[3], mate),
    ]

    cross_push = remote(wout_hbm, wout.at[1, half], push_send.at[5], push_recv.at[5], across)

    stage[...] = jnp.zeros_like(stage)
    diagonal = lax.broadcasted_iota(jnp.int32, (ROWS, HD), 0) == lax.broadcasted_iota(jnp.int32, (ROWS, HD), 1)
    lane = lax.broadcasted_iota(jnp.int32, (1, HD), 1)

    def put_squares(values, which):
        column = jnp.sum(values * values, axis=1, keepdims=True)
        row = jnp.sum(jnp.where(diagonal, column, 0.0), axis=0, keepdims=True)
        ss_send[which] = row
        ss_recv[which, s] = row

    def send_squares(which, d):
        remote(ss_send.at[which], ss_recv.at[which, s], ss_send_sem.at[which], ss_recv_sem.at[which],
               (side, shard_peer(d), t)).start()

    def squares_factor(which):
        wait_bytes(ss_recv.at[which, pl.ds(0, SHARDS - 1)], ss_recv_sem.at[which])
        return lax.rsqrt(jnp.sum(ss_recv[which], axis=0) / D + EPSILON)

    def turn_keys():
        for load in cache_loads:
            load.wait()
        eye = jnp.where(
            lax.broadcasted_iota(jnp.int32, (256, 256), 0) == lax.broadcasted_iota(jnp.int32, (256, 256), 1),
            1.0, 0.0).astype(BF)

        def turn(c):
            at = pl.ds(pl.multiple_of(512 * c, 512), 512)
            keys_t[:, at] = nt_dot(eye, kbuf[at, :]).astype(BF)

        loop(0, CTX // 512, turn)

    def attention():
        @pl.when(side == 0)
        def _():
            first_loads[0].wait()
            first_loads[1].wait()
            first_loads[2].wait()

        values = x_buf[...].astype(F32)
        put_squares(values, 2)
        mixed = jnp.dot((values * again[...]).astype(BF), wqkv[...], preferred_element_type=F32)
        for part in range(6):
            stage[pl.ds(part, ROWS, stride=8), :] = mixed[:, HD * part:HD * (part + 1)]
        send1[...] = stage[...].astype(BF).reshape(SHARDS, 16, HD)
        recv1[s] = send1[s]

        @pl.when(side == 0)
        def _():
            pl.semaphore_wait(barrier, SHARDS - 1)

        def go1(d):
            to = shard_peer(d)
            send_squares(2, d)
            remote(send1.at[to], recv1.at[s], send1_sem, recv1_sem, (side, to, t)).start()

        shard_peers(go1)

        @pl.when(side == 0)
        def _():
            first_loads[3].wait()
            first_loads[4].wait()
            turn_keys()
            pl.semaphore_wait(ready, 32)
            pushes[0].start()
            pushes[1].start()

        lens_here = [lens[2 * s + i] for i in range(2)]
        upper_row = lax.broadcasted_iota(jnp.int32, (16, 1), 0) >= 8
        position = jnp.where(upper_row, lens_here[1], lens_here[0])
        angle = position.astype(F32) * freq[...]
        cosine = jnp.cos(angle)
        sine = jnp.where(lane < HD // 2, -jnp.sin(angle), jnp.sin(angle))

        factor = squares_factor(2)
        scale_ref[0:1, :] = factor[:, :ROWS]
        own_factor = jnp.sum(
            jnp.where(lane == jnp.where(upper_row, 2 * s + 1, 2 * s), factor, 0.0), axis=1, keepdims=True)
        wait_bytes(recv1.at[pl.ds(0, SHARDS - 1)], recv1_sem)
        own = jnp.sum(recv1[...].astype(F32), axis=0) * own_factor
        rotated = own * cosine + pltpu.roll(own, HD // 2, 1) * sine
        rotated = rotated.astype(BF).astype(F32)
        own_values = own.astype(BF).astype(F32)
        new_key = jnp.concatenate(
            [jnp.broadcast_to(rotated[8 * i + 4:8 * i + 5], (8, HD)) for i in range(2)], axis=0)
        new_value = jnp.concatenate(
            [jnp.broadcast_to(own_values[8 * i + 5:8 * i + 6], (8, HD)) for i in range(2)], axis=0)
        own_score = jnp.sum(rotated * new_key, axis=1, keepdims=True) * HD ** (-0.5)
        both = jnp.concatenate(
            [jnp.where(upper_row, 0.0, rotated), jnp.where(upper_row, rotated, 0.0)], axis=1).astype(BF)

        tops, sums, parts = [], [], []
        for c in range(CTX // CHUNK):
            scores = jnp.dot(both, keys_t[:, CHUNK * c:CHUNK * (c + 1)], preferred_element_type=F32) * HD ** (-0.5)
            at = lax.broadcasted_iota(jnp.int32, (16, CHUNK), 1) + CHUNK * c
            scores = jnp.where(at < position, scores, -1e30)
            chunk_top = jnp.maximum(jnp.max(scores, axis=1, keepdims=True), own_score)
            weights = jnp.exp(scores - chunk_top)
            tops.append(chunk_top)
            sums.append(jnp.sum(weights, axis=1, keepdims=True))
            parts.append(jnp.dot(
                weights.astype(BF), vbuf[CHUNK * c:CHUNK * (c + 1), :], preferred_element_type=F32))
        top = functools.reduce(jnp.maximum, tops)
        own_weight = jnp.exp(own_score - top)
        total, mixed_values = own_weight, 0.0
        for chunk_top, chunk_sum, part in zip(tops, sums, parts):
            share = jnp.exp(chunk_top - top)
            total = total + share * chunk_sum
            mixed_values = mixed_values + share * part
        mixed_values = jnp.concatenate([mixed_values[:8, :HD], mixed_values[8:, HD:]], axis=0)
        mixed_values = mixed_values + own_weight.astype(BF).astype(F32) * new_value
        heads = mixed_values / total
        heads = jnp.concatenate([heads[0:4], heads[8:12]], axis=0).astype(BF)
        send2[...] = heads

        @pl.when(side == 1)
        def _():
            recv2[1, SHARDS * half + s] = heads

        def go2(dy, dz):
            @pl.when((side == 0) | (dy != 0) | (dz != 0))
            def _():
                remote(send2, recv2.at[side, SHARDS * half + s], send2_sem, recv2_sem.at[side],
                       plane_peer(1, dy, dz)).start()

        plane(go2)

    def prepare(slot):
        for load in gu_loads:
            load.wait()
        out_row = lax.broadcasted_iota(jnp.int32, (512, 512), 0)
        in_row = lax.broadcasted_iota(jnp.int32, (512, 512), 1)
        wanted = jnp.where(out_row < 256, 2 * out_row, 2 * (out_row - 256) + 1)
        pick = jnp.where(in_row == wanted, 1.0, 0.0).astype(BF)

        def one(o):
            for half in range(2):
                apart = jnp.dot(pick, graw[2 * o + half].reshape(512, HD), preferred_element_type=F32).astype(BF)
                wgu[slot, o, :, HD * half:HD * (half + 1)] = apart[:256]
                wgu[slot, o, :, 256 + HD * half:256 + HD * (half + 1)] = apart[256:]

        loop(0, OWNERS, one)

    owner = 2 * (s // 4) + s % 4 - 1
    owns = (s % 4 >= 1) & (s % 4 <= 2) & (owner < OWNERS)

    def layer(l):
        @pl.when(l == 0)
        def _():
            wait_bytes(wout.at[0, 0], push_recv.at[0])
            wait_bytes(wout.at[0, 0], push_recv.at[4])
            wait_bytes(recv2.at[0], recv2_sem.at[0])

        @pl.when(l == 1)
        def _():
            own_loads[2].wait()
            wait_bytes(wout.at[1, 0], push_recv.at[5])
            wait_bytes(recv2.at[1, pl.ds(0, 31)], recv2_sem.at[1])

        heads_f32[...] = recv2[l].astype(F32).reshape(256, HD)
        gathered = jnp.concatenate(
            [heads_f32[pl.ds(128 * h + g, ROWS, stride=4), :] for h in range(2) for g in range(4)], axis=1).astype(BF)
        projected = jnp.dot(gathered, wout[l].reshape(1024, 256), preferred_element_type=F32).astype(BF)
        send3[l] = projected
        recv3[l, x] = projected
        loop(1, 4, lambda d: remote(
            send3.at[l], recv3.at[l, x], send_sem.at[l, 0], recv_sem.at[l, 0], (1, s, x_peer(d))).start())

        @pl.when(l == 0)
        def _():
            cross_push.start()
            own_loads[0].wait()

        @pl.when(l == 1)
        def _():
            wait_bytes(fgain.at[1], push_recv.at[1])
            wait_bytes(wgu.at[1], push_recv.at[3])

        wait_bytes(recv3.at[l, pl.ds(0, 3)], recv_sem.at[l, 0])
        after = (x_buf[...].astype(F32) + jnp.sum(recv3[l].astype(F32), axis=0)).astype(BF)
        a_buf[...] = after
        values = after.astype(F32)
        put_squares(values, l)
        shard_peers(lambda d: send_squares(l, d))
        scaled = (values * fgain[l]).astype(BF)


        for d in range(OWNERS):
            o = lax.rem(jnp.where(owns, owner + 1, s) + d, OWNERS)
            both = jnp.dot(scaled, wgu[l, o], preferred_element_type=F32).astype(BF)
            send4[l, o] = both
            send = remote(send4.at[l, o], recv4.at[l, s], send_sem.at[l, 1], recv_sem.at[l, 1],
                          (1, 4 * (o // 2) + 1 + o % 2, t))
            if d < OWNERS - 1:
                send.start()
            else:
                pl.when(jnp.logical_not(owns))(send.start)

                @pl.when(owns)
                def _():
                    recv4[l, s] = both

        factor = squares_factor(l)
        column = jnp.sum(jnp.where(diagonal, factor, 0.0), axis=1, keepdims=True)

        @pl.when(owns)
        def _():
            wait_bytes(recv4.at[l, pl.ds(0, SHARDS - 1)], recv_sem.at[l, 1])
            both = jnp.sum(recv4[l].astype(F32), axis=0) * column
            gate, up = both[:, :256], both[:, 256:]
            hidden = (gate / (1.0 + jnp.exp(-gate)) * up).astype(BF)
            send5[l] = hidden
            recv5[l, owner] = hidden
            shard_peers(lambda d: remote(
                send5.at[l], recv5.at[l, owner], send_sem.at[l, 2], recv_sem.at[l, 2],
                (1, shard_peer(d), t)).start())

        @pl.when(l == 0)
        def _():
            scale_ref[1:2, :] = factor[:, :ROWS]
            own_loads[1].wait()

        @pl.when(l == 1)
        def _():
            end_scale[...] = factor
            remote(end_scale, end_scale, end_send.at[1], end_recv.at[1], mate).start()
            remote(a_buf, a_buf, end_send.at[0], end_recv.at[0], mate).start()
            wait_bytes(wdn.at[1], push_recv.at[2])

        @pl.when(owns)
        def _():
            wait_bytes(recv5.at[l, pl.ds(0, OWNERS - 1)], recv_sem.at[l, 2])

        @pl.when(jnp.logical_not(owns))
        def _():
            wait_bytes(recv5.at[l], recv_sem.at[l, 2])

        hidden_all = jnp.concatenate([recv5[l, o] for o in range(OWNERS)], axis=1)
        partial = jnp.dot(hidden_all, wdn[l], preferred_element_type=F32).astype(BF)
        send6[l] = partial

        @pl.when(l == 0)
        def _():
            recv6[t] = partial
            loop(1, TPS, lambda d: remote(
                send6.at[l], recv6.at[t], send_sem.at[l, 3], recv6_sem, (1, s, tp_peer(d))).start())
            wait_bytes(recv6.at[pl.ds(0, TPS - 1)], recv6_sem)
            result = (a_buf[...].astype(F32) + jnp.sum(recv6[...].astype(F32), axis=0)).astype(BF)
            x_buf[...] = result
            out_ref[...] = result

        @pl.when(l == 1)
        def _():
            loop(0, TPS, lambda d: remote(
                send6.at[l], recv6.at[t], send_sem.at[l, 3], recv6_sem, (0, s, tp_peer(d))).start())

    @pl.when(side == 1)
    def _():
        pl.semaphore_wait(barrier, 38 + 37)
        plane(lambda dy, dz: pl.semaphore_signal(
            ready, inc=1, device_id=plane_peer(0, dy, dz), device_id_type=MESH))
        prepare(0)
        for load in first_loads:
            load.wait()
        turn_keys()

    def step(l):
        pl.when(side == l)(attention)

        @pl.when(side == 1)
        def _():
            layer(l)

    loop(0, 2, step)

    wait_bytes(ss_recv.at[2, pl.ds(0, SHARDS - 1)], ss_send_sem.at[2])
    wait_bytes(recv1.at[pl.ds(0, SHARDS - 1)], send1_sem)

    @pl.when(side == 0)
    def _():
        prepare(1)
        for push in pushes[2:]:
            push.start()
        wait_bytes(recv2.at[0], send2_sem)
        for push in pushes:
            push.wait_send()
        wait_bytes(end_scale, end_recv.at[1])
        scale_ref[1:2, :] = end_scale[:, :ROWS]
        wait_bytes(a_buf, end_recv.at[0])
        wait_bytes(recv6, recv6_sem)
        out_ref[...] = (a_buf[...].astype(F32) + jnp.sum(recv6[...].astype(F32), axis=0)).astype(BF)

    @pl.when(side == 1)
    def _():
        wait_bytes(recv2.at[1, pl.ds(0, 31)], send2_sem)
        cross_push.wait_send()

        def sent(l):
            wait_bytes(ss_recv.at[l, pl.ds(0, SHARDS - 1)], ss_send_sem.at[l])
            wait_bytes(recv3.at[l, pl.ds(0, 3)], send_sem.at[l, 0])

            @pl.when(owns)
            def _():
                wait_bytes(recv4.at[l, pl.ds(0, OWNERS - 1)], send_sem.at[l, 1])
                wait_bytes(recv4.at[l, pl.ds(0, SHARDS - 1), :, pl.ds(0, 256)], send_sem.at[l, 2])

            @pl.when(jnp.logical_not(owns))
            def _():
                wait_bytes(recv4.at[l, pl.ds(0, OWNERS)], send_sem.at[l, 1])

        loop(0, 2, sent)
        wait_bytes(recv6.at[pl.ds(0, TPS - 1)], send_sem.at[0, 3])
        wait_bytes(recv6, send_sem.at[1, 3])
        wait_bytes(a_buf, end_send.at[0])
        wait_bytes(end_scale, end_send.at[1])


def body(tokens, lengths, kv_cache, attn_gain, qkv_weight, out_weight, ffn_gain, gate_up, down_weight):
    freqs = (ROPE_BASE ** (-np.arange(HD // 2, dtype=np.float64) * 2.0 / HD)).astype(np.float32)
    freqs = jnp.asarray(np.concatenate([freqs, freqs])[None])
    vmem = pl.BlockSpec(memory_space=pltpu.VMEM)
    hbm = pl.BlockSpec(memory_space=pltpu.HBM)
    dma = pltpu.SemaphoreType.DMA
    out, scales = pl.pallas_call(
        kernel,
        out_shape=(pltpu.VMEM((ROWS, 256), BF), pltpu.VMEM((2, ROWS), F32)),
        in_specs=[hbm] * 10,
        out_specs=(vmem, vmem),
        scratch_shapes=[
            pltpu.SMEM((ROWS,), jnp.int32),
            pltpu.VMEM((1, 256), F32), pltpu.VMEM((2, 1, 256), F32), pltpu.VMEM((1, HD), F32),
            pltpu.VMEM((CTX, 2 * HD), BF), pltpu.VMEM((CTX, 2 * HD), BF), pltpu.VMEM((2 * HD, CTX), BF),
            pltpu.VMEM((256, 768), BF), pltpu.VMEM((2, 2, 512, 256), BF),
            pltpu.VMEM((TILES, 256, 2, HD), BF), pltpu.VMEM((2, OWNERS, 256, 512), BF),
            pltpu.VMEM((2, TILES * HD, 256), BF),
            pltpu.VMEM((ROWS, 256), BF), pltpu.VMEM((ROWS, 256), BF),
            pltpu.VMEM((3, 1, HD), F32), pltpu.VMEM((3, SHARDS, 1, HD), F32),
            pltpu.VMEM((16 * SHARDS, HD), F32), pltpu.VMEM((SHARDS, 16, HD), BF), pltpu.VMEM((SHARDS, 16, HD), BF),
            pltpu.VMEM((8, HD), BF), pltpu.VMEM((2, 2 * SHARDS, 8, HD), BF), pltpu.VMEM((256, HD), F32),
            pltpu.VMEM((2, ROWS, 256), BF), pltpu.VMEM((2, 4, ROWS, 256), BF),
            pltpu.VMEM((2, OWNERS, ROWS, 512), BF), pltpu.VMEM((2, SHARDS, ROWS, 512), BF),
            pltpu.VMEM((2, ROWS, 256), BF), pltpu.VMEM((2, OWNERS, ROWS, 256), BF),
            pltpu.VMEM((2, ROWS, 256), BF), pltpu.VMEM((TPS, ROWS, 256), BF),
            pltpu.VMEM((1, HD), F32),
            dma((12,)), dma((TILES,)), dma((3,)), dma((3,)), dma, dma, dma, dma((2,)),
            dma((2, 4)), dma((2, 3)), dma, dma((6,)), dma((6,)), dma((2,)), dma((2,)),
            pltpu.SemaphoreType.REGULAR,
        ],
        compiler_params=pltpu.CompilerParams(
            collective_id=0, has_side_effects=True, vmem_limit_bytes=63 * 1024 * 1024),
        cost_estimate=pl.CostEstimate(flops=130_000_000, bytes_accessed=7_500_000, transcendentals=70_000),
    )(*(pltpu.with_memory_space_constraint(x, pltpu.HBM) for x in (
        tokens, lengths, attn_gain, ffn_gain, freqs,
        kv_cache.reshape(2, CTX, 2 * HD), qkv_weight.reshape(256, 768), out_weight.reshape(512, 256),
        gate_up.reshape(256, 2, 1792), down_weight.reshape(1792, 256),
    )))
    return (out[None], scales[None])


def solution(mesh):
    in_specs = (
        P(None, "shard"),
        P(),
        P("side", "shard", None, "tp", None),
        P("side", "shard"),
        P("side", "shard", "tp", None),
        P("side", "tp", None, "shard"),
        P("side", "shard"),
        P("side", "shard", None, "tp"),
        P("side", "tp", "shard"),
    )
    out_specs = (P("side", None, "shard"), P("side", None, None))
    return jax.shard_map(body, mesh=mesh, in_specs=in_specs, out_specs=out_specs, check_vma=False)
```

```python
import functools

import jax
import jax.numpy as jnp
import numpy as np
from jax import lax
from jax.experimental import pallas as pl
from jax.experimental.pallas import tpu as pltpu
from jax.sharding import PartitionSpec as P

D = 4096
HD = 128
ROWS = 32
EPSILON = 1e-05
ROPE_BASE = 500000.0
SHARDS = 16
TPS = 8
TILES = 14
OWNERS = 7
CTX = 4096
CHUNK = 1024
BF = jnp.bfloat16
F32 = jnp.float32
MESH = pl.DeviceIdType.MESH


def nt_dot(a, b):
    return lax.dot_general(a, b, (((1,), (1,)), ((), ())), preferred_element_type=F32)


def wait_bytes(ref, sem):
    pltpu.make_async_copy(ref, ref, sem).wait()


def remote(src, dst, ssem, rsem, device):
    return pltpu.make_async_remote_copy(
        src_ref=src, dst_ref=dst, send_sem=ssem, recv_sem=rsem, device_id=device, device_id_type=MESH)


def kernel(
    tok_hbm, lens_hbm, again_hbm, fgain_hbm, freq_hbm, cache_hbm, wqkv_hbm, wout_hbm, wgu_hbm, wdn_hbm,
    out_ref, scale_ref,
    lens, again, fgain, freq,
    kbuf, vbuf, keys_t, wqkv, wout, graw, wgu, wdn,
    x_buf, a_buf,
    ss_send, ss_recv, stage, send1, recv1, send2, recv2, heads_f32,
    send3, recv3, send4, recv4, send5, recv5, send6, recv6, end_scale,
    load_sem, gu_sem, ss_send_sem, ss_recv_sem, send1_sem, recv1_sem, send2_sem, recv2_sem,
    send_sem, recv_sem, recv6_sem, push_send, push_recv, end_send, end_recv,
):
    side = lax.axis_index("side")
    s = lax.axis_index("shard")
    t = lax.axis_index("tp")
    mate = (1 - side, s, t)

    def shard_peer(d):
        return lax.rem(s + d, SHARDS)

    def tp_peer(d):
        return lax.rem(t + d, TPS)

    barrier = pltpu.get_barrier_semaphore()

    def greet(device):
        pl.semaphore_signal(barrier, inc=1, device_id=device, device_id_type=MESH)

    def loop(start, stop, step):
        def go(d, carry):
            step(d)
            return carry

        lax.fori_loop(start, stop, go, 0)

    @pl.when(side == 0)
    def _():
        loop(1, SHARDS, lambda d: greet((0, shard_peer(d), t)))
        loop(0, TPS, lambda d: greet((1, s, tp_peer(d))))

    @pl.when(side == 1)
    def _():
        loop(0, SHARDS, lambda d: greet((0, shard_peer(d), t)))
        loop(1, SHARDS, lambda d: greet((1, shard_peer(d), t)))
        loop(1, TPS, lambda d: greet((1, s, tp_peer(d))))

    first_loads = [
        pltpu.make_async_copy(tok_hbm, x_buf, load_sem.at[0]),
        pltpu.make_async_copy(again_hbm, again, load_sem.at[1]),
        pltpu.make_async_copy(wqkv_hbm, wqkv, load_sem.at[2]),
        pltpu.make_async_copy(lens_hbm, lens, load_sem.at[3]),
        pltpu.make_async_copy(freq_hbm, freq, load_sem.at[4]),
    ]
    cache_loads = []
    for i in range(2):
        cache_loads.append(pltpu.make_async_copy(
            cache_hbm.at[i, :, pl.ds(0, HD)], kbuf.at[:, pl.ds(HD * i, HD)], load_sem.at[5 + i]))
        cache_loads.append(pltpu.make_async_copy(
            cache_hbm.at[i, :, pl.ds(HD, HD)], vbuf.at[:, pl.ds(HD * i, HD)], load_sem.at[7 + i]))
    own_loads = [
        pltpu.make_async_copy(fgain_hbm, fgain.at[0], load_sem.at[9]),
        pltpu.make_async_copy(wdn_hbm, wdn.at[0], load_sem.at[10]),
        pltpu.make_async_copy(wout_hbm, wout.at[side], load_sem.at[11]),
    ]
    gu_loads = [
        pltpu.make_async_copy(wgu_hbm.at[:, :, pl.ds(HD * j, HD)], graw.at[j], gu_sem.at[j]) for j in range(TILES)
    ]
    for load in first_loads:
        load.start()
    own_loads[2].start()

    @pl.when(side == 0)
    def _():
        for load in cache_loads:
            load.start()

    for load in gu_loads:
        load.start()

    @pl.when(side == 1)
    def _():
        for load in own_loads[:2]:
            load.start()
        for load in cache_loads:
            load.start()

    pushes = [
        remote(wout.at[0], wout.at[0], push_send.at[0], push_recv.at[0], mate),
        remote(fgain_hbm, fgain.at[1], push_send.at[1], push_recv.at[1], mate),
        remote(wdn_hbm, wdn.at[1], push_send.at[2], push_recv.at[2], mate),
        remote(wgu.at[1], wgu.at[1], push_send.at[3], push_recv.at[3], mate),
    ]

    diagonal = lax.broadcasted_iota(jnp.int32, (ROWS, HD), 0) == lax.broadcasted_iota(jnp.int32, (ROWS, HD), 1)
    lane = lax.broadcasted_iota(jnp.int32, (1, HD), 1)

    def put_squares(values, which):
        column = jnp.sum(values * values, axis=1, keepdims=True)
        row = jnp.sum(jnp.where(diagonal, column, 0.0), axis=0, keepdims=True)
        ss_send[which] = row
        ss_recv[which, s] = row

    def send_squares(which, d):
        remote(ss_send.at[which], ss_recv.at[which, s], ss_send_sem.at[which], ss_recv_sem.at[which],
               (side, shard_peer(d), t)).start()

    def squares_factor(which):
        wait_bytes(ss_recv.at[which, pl.ds(0, SHARDS - 1)], ss_recv_sem.at[which])
        return lax.rsqrt(jnp.sum(ss_recv[which], axis=0) / D + EPSILON)

    def turn_keys():
        for load in cache_loads:
            load.wait()
        eye = jnp.where(
            lax.broadcasted_iota(jnp.int32, (256, 256), 0) == lax.broadcasted_iota(jnp.int32, (256, 256), 1),
            1.0, 0.0).astype(BF)

        def turn(c):
            at = pl.ds(pl.multiple_of(512 * c, 512), 512)
            keys_t[:, at] = nt_dot(eye, kbuf[at, :]).astype(BF)

        loop(0, CTX // 512, turn)

    def attention():
        @pl.when(side == 0)
        def _():
            first_loads[0].wait()
            first_loads[1].wait()
            first_loads[2].wait()

        values = x_buf[...].astype(F32)
        put_squares(values, 2)
        mixed = jnp.dot((values * again[...]).astype(BF), wqkv[...], preferred_element_type=F32)
        for part in range(6):
            stage[pl.ds(part, ROWS, stride=8), :] = mixed[:, HD * part:HD * (part + 1)]
        column = jnp.broadcast_to(jnp.sum(values * values, axis=1, keepdims=True), (ROWS, HD))
        rounded = column.astype(BF).astype(F32)
        stage[pl.ds(6, ROWS, stride=8), :] = rounded
        stage[pl.ds(7, ROWS, stride=8), :] = column - rounded
        send1[...] = stage[...].astype(BF).reshape(SHARDS, 16, HD)
        recv1[s] = send1[s]

        @pl.when(side == 0)
        def _():
            pl.semaphore_wait(barrier, 2 * SHARDS - 1)

        def go1(d):
            to = shard_peer(d)
            remote(send1.at[to], recv1.at[s], send1_sem, recv1_sem, (side, to, t)).start()

        loop(1, SHARDS, go1)
        loop(1, SHARDS, lambda d: send_squares(2, d))

        @pl.when(side == 0)
        def _():
            own_loads[2].wait()
            pushes[0].start()
            first_loads[3].wait()
            first_loads[4].wait()
            turn_keys()

        lens_here = [lens[2 * s + i] for i in range(2)]
        upper_row = lax.broadcasted_iota(jnp.int32, (16, 1), 0) >= 8
        position = jnp.where(upper_row, lens_here[1], lens_here[0])
        angle = position.astype(F32) * freq[...]
        cosine = jnp.cos(angle)
        sine = jnp.where(lane < HD // 2, -jnp.sin(angle), jnp.sin(angle))

        wait_bytes(recv1.at[pl.ds(0, SHARDS - 1)], recv1_sem)
        own = jnp.sum(recv1[...].astype(F32), axis=0)
        squares = jnp.concatenate(
            [jnp.broadcast_to(own[8 * i + 6:8 * i + 7] + own[8 * i + 7:8 * i + 8], (8, HD)) for i in range(2)], axis=0)
        own = own * lax.rsqrt(squares / D + EPSILON)
        rotated = own * cosine + pltpu.roll(own, HD // 2, 1) * sine
        rotated = rotated.astype(BF).astype(F32)
        own_values = own.astype(BF).astype(F32)
        new_key = jnp.concatenate(
            [jnp.broadcast_to(rotated[8 * i + 4:8 * i + 5], (8, HD)) for i in range(2)], axis=0)
        new_value = jnp.concatenate(
            [jnp.broadcast_to(own_values[8 * i + 5:8 * i + 6], (8, HD)) for i in range(2)], axis=0)
        own_score = jnp.sum(rotated * new_key, axis=1, keepdims=True) * HD ** (-0.5)
        both = jnp.concatenate(
            [jnp.where(upper_row, 0.0, rotated), jnp.where(upper_row, rotated, 0.0)], axis=1).astype(BF)

        tops, sums, parts = [], [], []
        for c in range(CTX // CHUNK):
            scores = jnp.dot(both, keys_t[:, CHUNK * c:CHUNK * (c + 1)], preferred_element_type=F32) * HD ** (-0.5)
            at = lax.broadcasted_iota(jnp.int32, (16, CHUNK), 1) + CHUNK * c
            scores = jnp.where(at < position, scores, -1e30)
            chunk_top = jnp.maximum(jnp.max(scores, axis=1, keepdims=True), own_score)
            weights = jnp.exp(scores - chunk_top)
            tops.append(chunk_top)
            sums.append(jnp.sum(weights, axis=1, keepdims=True))
            parts.append(jnp.dot(
                weights.astype(BF), vbuf[CHUNK * c:CHUNK * (c + 1), :], preferred_element_type=F32))
        top = functools.reduce(jnp.maximum, tops)
        own_weight = jnp.exp(own_score - top)
        total, mixed_values = own_weight, 0.0
        for chunk_top, chunk_sum, part in zip(tops, sums, parts):
            share = jnp.exp(chunk_top - top)
            total = total + share * chunk_sum
            mixed_values = mixed_values + share * part
        mixed_values = jnp.concatenate([mixed_values[:8, :HD], mixed_values[8:, HD:]], axis=0)
        mixed_values = mixed_values + own_weight.astype(BF).astype(F32) * new_value
        heads = mixed_values / total
        heads = jnp.concatenate([heads[0:4], heads[8:12]], axis=0).astype(BF)
        send2[...] = heads

        @pl.when(side == 1)
        def _():
            recv2[1, s] = heads

        @pl.when(side == 0)
        def _():
            remote(send2, recv2.at[side, s], send2_sem, recv2_sem.at[side], mate).start()

        loop(1, SHARDS, lambda d: remote(
            send2, recv2.at[side, s], send2_sem, recv2_sem.at[side], (1, shard_peer(d), t)).start())
        scale_ref[0:1, :] = squares_factor(2)[:, :ROWS]

    def prepare(slot):
        for load in gu_loads:
            load.wait()
        out_row = lax.broadcasted_iota(jnp.int32, (512, 512), 0)
        in_row = lax.broadcasted_iota(jnp.int32, (512, 512), 1)
        wanted = jnp.where(out_row < 256, 2 * out_row, 2 * (out_row - 256) + 1)
        pick = jnp.where(in_row == wanted, 1.0, 0.0).astype(BF)

        def one(o):
            raw = jnp.concatenate([graw[2 * o].reshape(512, HD), graw[2 * o + 1].reshape(512, HD)], axis=1)
            apart = jnp.dot(pick, raw, preferred_element_type=F32).astype(BF)
            for part in range(4):
                wgu[slot, o, :, HD * part:HD * (part + 1)] = apart[
                    256 * (part % 2):256 * (part % 2 + 1), HD * (part // 2):HD * (part // 2 + 1)]

        loop(0, OWNERS, one)

    owner = 2 * (s // 4) + s % 4 - 1
    owns = (s % 4 >= 1) & (s % 4 <= 2) & (owner < OWNERS)

    def layer(l):
        @pl.when(l == 0)
        def _():
            wait_bytes(wout.at[0], push_recv.at[0])
            wait_bytes(recv2.at[0], recv2_sem.at[0])

        @pl.when(l == 1)
        def _():
            own_loads[2].wait()
            wait_bytes(recv2.at[1, pl.ds(0, SHARDS - 1)], recv2_sem.at[1])

        heads_f32[...] = recv2[l].astype(F32).reshape(8 * SHARDS, HD)
        gathered = jnp.concatenate(
            [heads_f32[pl.ds(g, ROWS, stride=4), :] for g in range(4)], axis=1).astype(BF)
        projected = jnp.dot(gathered, wout[l], preferred_element_type=F32).astype(BF)
        send3[l] = projected
        recv3[l, t] = projected
        loop(1, TPS, lambda d: remote(
            send3.at[l], recv3.at[l, t], send_sem.at[l, 0], recv_sem.at[l, 0], (1, s, tp_peer(d))).start())

        @pl.when(l == 0)
        def _():
            own_loads[0].wait()

        @pl.when(l == 1)
        def _():
            wait_bytes(fgain.at[1], push_recv.at[1])
            wait_bytes(wgu.at[1], push_recv.at[3])

        wait_bytes(recv3.at[l, pl.ds(0, TPS - 1)], recv_sem.at[l, 0])
        after = (x_buf[...].astype(F32) + jnp.sum(recv3[l].astype(F32), axis=0)).astype(BF)
        a_buf[...] = after
        values = after.astype(F32)
        put_squares(values, l)
        scaled = (values * fgain[l]).astype(BF)

        for part in range(2):
            for d in range(OWNERS):
                o = lax.rem(jnp.where(owns, owner + 1, s) + d, OWNERS)
                both = jnp.dot(scaled, wgu[l, o, :, 256 * part:256 * (part + 1)], preferred_element_type=F32).astype(BF)
                send4[l, part, o] = both
                send = remote(send4.at[l, part, o], recv4.at[l, part, s], send_sem.at[l, 1 + part],
                              recv_sem.at[l, 1 + part], (1, 4 * (o // 2) + 1 + o % 2, t))
                if d < OWNERS - 1:
                    send.start()
                else:
                    pl.when(jnp.logical_not(owns))(send.start)

                    @pl.when(owns)
                    def _():
                        recv4[l, part, s] = both

            if part == 0:
                loop(1, SHARDS, lambda d: send_squares(l, d))

        pl.when(l == 0)(turn_keys)
        factor = squares_factor(l)
        column = jnp.sum(jnp.where(diagonal, factor, 0.0), axis=1, keepdims=True)

        @pl.when(owns)
        def _():
            for part in range(2):
                wait_bytes(recv4.at[l, part, pl.ds(0, SHARDS - 1)], recv_sem.at[l, 1 + part])
                both = jnp.sum(recv4[l, part].astype(F32), axis=0) * column
                gate, up = both[:, :HD], both[:, HD:]
                hidden = (gate / (1.0 + jnp.exp(-gate)) * up).astype(BF)
                send5[l, part] = hidden
                recv5[l, owner, part] = hidden
                loop(1, SHARDS, lambda d: remote(
                    send5.at[l, part], recv5.at[l, owner, part], send_sem.at[l, 3], recv_sem.at[l, 3],
                    (1, shard_peer(d), t)).start())

        @pl.when(l == 0)
        def _():
            scale_ref[1:2, :] = factor[:, :ROWS]
            own_loads[1].wait()

        @pl.when(l == 1)
        def _():
            end_scale[...] = factor
            remote(end_scale, end_scale, end_send.at[1], end_recv.at[1], mate).start()
            remote(a_buf, a_buf, end_send.at[0], end_recv.at[0], mate).start()
            wait_bytes(wdn.at[1], push_recv.at[2])

        @pl.when(owns)
        def _():
            wait_bytes(recv5.at[l, pl.ds(0, OWNERS - 1)], recv_sem.at[l, 3])

        @pl.when(jnp.logical_not(owns))
        def _():
            wait_bytes(recv5.at[l], recv_sem.at[l, 3])

        hidden_all = jnp.concatenate([recv5[l, o, part] for o in range(OWNERS) for part in range(2)], axis=1)
        partial = jnp.dot(hidden_all, wdn[l], preferred_element_type=F32).astype(BF)
        send6[l] = partial

        @pl.when(l == 0)
        def _():
            recv6[t] = partial
            loop(1, TPS, lambda d: remote(
                send6.at[l], recv6.at[t], send_sem.at[l, 4], recv6_sem, (1, s, tp_peer(d))).start())
            wait_bytes(recv6.at[pl.ds(0, TPS - 1)], recv6_sem)
            result = (a_buf[...].astype(F32) + jnp.sum(recv6[...].astype(F32), axis=0)).astype(BF)
            x_buf[...] = result
            out_ref[...] = result

        @pl.when(l == 1)
        def _():
            loop(0, TPS, lambda d: remote(
                send6.at[l], recv6.at[t], send_sem.at[l, 4], recv6_sem, (0, s, tp_peer(d))).start())

    @pl.when(side == 1)
    def _():
        prepare(0)
        for load in first_loads:
            load.wait()
        pl.semaphore_wait(barrier, SHARDS - 1 + TPS - 1 + TPS)

    def step(l):
        pl.when(side == l)(attention)

        @pl.when(side == 1)
        def _():
            layer(l)

    loop(0, 2, step)

    wait_bytes(ss_recv.at[2, pl.ds(0, SHARDS - 1)], ss_send_sem.at[2])
    wait_bytes(recv1.at[pl.ds(0, SHARDS - 1)], send1_sem)

    @pl.when(side == 0)
    def _():
        prepare(1)
        for push in pushes[1:]:
            push.start()
        wait_bytes(recv2.at[0], send2_sem)
        for push in pushes:
            push.wait_send()
        wait_bytes(end_scale, end_recv.at[1])
        scale_ref[1:2, :] = end_scale[:, :ROWS]
        wait_bytes(a_buf, end_recv.at[0])
        wait_bytes(recv6, recv6_sem)
        out_ref[...] = (a_buf[...].astype(F32) + jnp.sum(recv6[...].astype(F32), axis=0)).astype(BF)

    @pl.when(side == 1)
    def _():
        wait_bytes(recv2.at[1, pl.ds(0, SHARDS - 1)], send2_sem)

        def sent(l):
            wait_bytes(ss_recv.at[l, pl.ds(0, SHARDS - 1)], ss_send_sem.at[l])
            wait_bytes(recv3.at[l, pl.ds(0, TPS - 1)], send_sem.at[l, 0])

            for part in range(2):
                @pl.when(owns)
                def _():
                    wait_bytes(recv4.at[l, part, pl.ds(0, OWNERS - 1)], send_sem.at[l, 1 + part])

                @pl.when(jnp.logical_not(owns))
                def _():
                    wait_bytes(recv4.at[l, part, pl.ds(0, OWNERS)], send_sem.at[l, 1 + part])

            @pl.when(owns)
            def _():
                wait_bytes(recv4.at[l, 0, pl.ds(0, SHARDS - 1)], send_sem.at[l, 3])

        loop(0, 2, sent)
        wait_bytes(recv6.at[pl.ds(0, TPS - 1)], send_sem.at[0, 4])
        wait_bytes(recv6, send_sem.at[1, 4])
        wait_bytes(a_buf, end_send.at[0])
        wait_bytes(end_scale, end_send.at[1])


def body(tokens, lengths, kv_cache, attn_gain, qkv_weight, out_weight, ffn_gain, gate_up, down_weight):
    freqs = (ROPE_BASE ** (-np.arange(HD // 2, dtype=np.float64) * 2.0 / HD)).astype(np.float32)
    freqs = jnp.asarray(np.concatenate([freqs, freqs])[None])
    vmem = pl.BlockSpec(memory_space=pltpu.VMEM)
    hbm = pl.BlockSpec(memory_space=pltpu.HBM)
    dma = pltpu.SemaphoreType.DMA
    out, scales = pl.pallas_call(
        kernel,
        out_shape=(pltpu.VMEM((ROWS, 256), BF), pltpu.VMEM((2, ROWS), F32)),
        in_specs=[hbm] * 10,
        out_specs=(vmem, vmem),
        scratch_shapes=[
            pltpu.SMEM((ROWS,), jnp.int32),
            pltpu.VMEM((1, 256), F32), pltpu.VMEM((2, 1, 256), F32), pltpu.VMEM((1, HD), F32),
            pltpu.VMEM((CTX, 2 * HD), BF), pltpu.VMEM((CTX, 2 * HD), BF), pltpu.VMEM((2 * HD, CTX), BF),
            pltpu.VMEM((256, 768), BF), pltpu.VMEM((2, 512, 256), BF),
            pltpu.VMEM((TILES, 256, 2, HD), BF), pltpu.VMEM((2, OWNERS, 256, 512), BF),
            pltpu.VMEM((2, TILES * HD, 256), BF),
            pltpu.VMEM((ROWS, 256), BF), pltpu.VMEM((ROWS, 256), BF),
            pltpu.VMEM((3, 1, HD), F32), pltpu.VMEM((3, SHARDS, 1, HD), F32),
            pltpu.VMEM((16 * SHARDS, HD), F32), pltpu.VMEM((SHARDS, 16, HD), BF), pltpu.VMEM((SHARDS, 16, HD), BF),
            pltpu.VMEM((8, HD), BF), pltpu.VMEM((2, SHARDS, 8, HD), BF), pltpu.VMEM((8 * SHARDS, HD), F32),
            pltpu.VMEM((2, ROWS, 256), BF), pltpu.VMEM((2, TPS, ROWS, 256), BF),
            pltpu.VMEM((2, 2, OWNERS, ROWS, 256), BF), pltpu.VMEM((2, 2, SHARDS, ROWS, 256), BF),
            pltpu.VMEM((2, 2, ROWS, HD), BF), pltpu.VMEM((2, OWNERS, 2, ROWS, HD), BF),
            pltpu.VMEM((2, ROWS, 256), BF), pltpu.VMEM((TPS, ROWS, 256), BF),
            pltpu.VMEM((1, HD), F32),
            dma((12,)), dma((TILES,)), dma((3,)), dma((3,)), dma, dma, dma, dma((2,)),
            dma((2, 5)), dma((2, 4)), dma, dma((4,)), dma((4,)), dma((2,)), dma((2,)),
        ],
        compiler_params=pltpu.CompilerParams(
            collective_id=0, has_side_effects=True, vmem_limit_bytes=63 * 1024 * 1024),
        cost_estimate=pl.CostEstimate(flops=130_000_000, bytes_accessed=7_500_000, transcendentals=70_000),
    )(*(pltpu.with_memory_space_constraint(x, pltpu.HBM) for x in (
        tokens, lengths, attn_gain, ffn_gain, freqs,
        kv_cache.reshape(2, CTX, 2 * HD), qkv_weight.reshape(256, 768), out_weight.reshape(512, 256),
        gate_up.reshape(256, 2, 1792), down_weight.reshape(1792, 256),
    )))
    return (out[None], scales[None])


def solution(mesh):
    in_specs = (
        P(None, "shard"),
        P(),
        P("side", "shard", None, "tp", None),
        P("side", "shard"),
        P("side", "shard", "tp", None),
        P("side", "tp", None, "shard"),
        P("side", "shard"),
        P("side", "shard", None, "tp"),
        P("side", "tp", "shard"),
    )
    out_specs = (P("side", None, "shard"), P("side", None, None))
    return jax.shard_map(body, mesh=mesh, in_specs=in_specs, out_specs=out_specs, check_vma=False)
```

```python
import functools

import jax
import jax.numpy as jnp
import numpy as np
from jax import lax
from jax.experimental import pallas as pl
from jax.experimental.pallas import tpu as pltpu
from jax.sharding import PartitionSpec as P

D = 4096
HD = 128
ROWS = 32
EPSILON = 1e-05
ROPE_BASE = 500000.0
SHARDS = 16
TPS = 8
TILES = 14
OWNERS = 7
CTX = 4096
CHUNK = 1024
BF = jnp.bfloat16
F32 = jnp.float32
MESH = pl.DeviceIdType.MESH


def nt_dot(a, b):
    return lax.dot_general(a, b, (((1,), (1,)), ((), ())), preferred_element_type=F32)


def wait_bytes(ref, sem):
    pltpu.make_async_copy(ref, ref, sem).wait()


def remote(src, dst, ssem, rsem, device):
    return pltpu.make_async_remote_copy(
        src_ref=src, dst_ref=dst, send_sem=ssem, recv_sem=rsem, device_id=device, device_id_type=MESH)


def kernel(
    tok_hbm, lens_hbm, again_hbm, fgain_hbm, freq_hbm, cache_hbm, wqkv_hbm, wout_hbm, wgu_hbm, wdn_hbm,
    out_ref, scale_ref,
    lens, again, fgain, freq,
    kbuf, vbuf, keys_t, wqkv, wout, graw, wgu, wdn,
    x_buf, a_buf,
    ss_send, ss_recv, stage, send1, recv1, send2, recv2, heads_f32,
    send3, recv3, send4, recv4, send5, recv5, send6, recv6, end_scale,
    load_sem, gu_sem, ss_send_sem, ss_recv_sem, send1_sem, recv1_sem, send2_sem, recv2_sem,
    send_sem, recv_sem, recv6_sem, push_send, push_recv, end_send, end_recv,
):
    side = lax.axis_index("side")
    s = lax.axis_index("shard")
    t = lax.axis_index("tp")
    mate = (1 - side, s, t)

    def shard_peer(d):
        return lax.rem(s + d, SHARDS)

    def tp_peer(d):
        return lax.rem(t + d, TPS)

    barrier = pltpu.get_barrier_semaphore()

    def greet(device):
        pl.semaphore_signal(barrier, inc=1, device_id=device, device_id_type=MESH)

    def loop(start, stop, step):
        def go(d, carry):
            step(d)
            return carry

        lax.fori_loop(start, stop, go, 0)

    @pl.when(side == 0)
    def _():
        loop(1, SHARDS, lambda d: greet((0, shard_peer(d), t)))
        loop(0, TPS, lambda d: greet((1, s, tp_peer(d))))

    @pl.when(side == 1)
    def _():
        greet(mate)
        loop(1, SHARDS, lambda d: greet((1, shard_peer(d), t)))
        loop(1, TPS, lambda d: greet((1, s, tp_peer(d))))

    first_loads = [
        pltpu.make_async_copy(tok_hbm, x_buf, load_sem.at[0]),
        pltpu.make_async_copy(again_hbm, again, load_sem.at[1]),
        pltpu.make_async_copy(wqkv_hbm, wqkv, load_sem.at[2]),
        pltpu.make_async_copy(lens_hbm, lens, load_sem.at[3]),
        pltpu.make_async_copy(freq_hbm, freq, load_sem.at[4]),
    ]
    cache_loads = []
    for i in range(2):
        cache_loads.append(pltpu.make_async_copy(
            cache_hbm.at[i, :, pl.ds(0, HD)], kbuf.at[:, pl.ds(HD * i, HD)], load_sem.at[5 + i]))
        cache_loads.append(pltpu.make_async_copy(
            cache_hbm.at[i, :, pl.ds(HD, HD)], vbuf.at[:, pl.ds(HD * i, HD)], load_sem.at[7 + i]))
    own_loads = [
        pltpu.make_async_copy(fgain_hbm, fgain.at[0], load_sem.at[9]),
        pltpu.make_async_copy(wdn_hbm, wdn.at[0], load_sem.at[10]),
        pltpu.make_async_copy(wout_hbm, wout.at[side], load_sem.at[11]),
    ]
    gu_loads = [
        pltpu.make_async_copy(wgu_hbm.at[:, :, pl.ds(HD * j, HD)], graw.at[j], gu_sem.at[j]) for j in range(TILES)
    ]
    for load in first_loads:
        load.start()
    own_loads[2].start()

    @pl.when(side == 0)
    def _():
        for load in cache_loads:
            load.start()

    for load in gu_loads:
        load.start()

    @pl.when(side == 1)
    def _():
        for load in own_loads[:2]:
            load.start()
        for load in cache_loads:
            load.start()

    pushes = [
        remote(wout.at[0], wout.at[0], push_send.at[0], push_recv.at[0], mate),
        remote(fgain_hbm, fgain.at[1], push_send.at[1], push_recv.at[1], mate),
        remote(wdn_hbm, wdn.at[1], push_send.at[2], push_recv.at[2], mate),
        remote(wgu.at[1], wgu.at[1], push_send.at[3], push_recv.at[3], mate),
    ]

    diagonal = lax.broadcasted_iota(jnp.int32, (ROWS, HD), 0) == lax.broadcasted_iota(jnp.int32, (ROWS, HD), 1)
    lane = lax.broadcasted_iota(jnp.int32, (1, HD), 1)

    def put_squares(values, which):
        column = jnp.sum(values * values, axis=1, keepdims=True)
        row = jnp.sum(jnp.where(diagonal, column, 0.0), axis=0, keepdims=True)
        ss_send[which] = row
        ss_recv[which, s] = row

    def send_squares(which, d):
        remote(ss_send.at[which], ss_recv.at[which, s], ss_send_sem.at[which], ss_recv_sem.at[which],
               (side, shard_peer(d), t)).start()

    def squares_factor(which):
        wait_bytes(ss_recv.at[which, pl.ds(0, SHARDS - 1)], ss_recv_sem.at[which])
        return lax.rsqrt(jnp.sum(ss_recv[which], axis=0) / D + EPSILON)

    def turn_keys():
        for load in cache_loads:
            load.wait()
        eye = jnp.where(
            lax.broadcasted_iota(jnp.int32, (256, 256), 0) == lax.broadcasted_iota(jnp.int32, (256, 256), 1),
            1.0, 0.0).astype(BF)

        def turn(c):
            at = pl.ds(pl.multiple_of(512 * c, 512), 512)
            keys_t[:, at] = nt_dot(eye, kbuf[at, :]).astype(BF)

        loop(0, CTX // 512, turn)

    def attention():
        @pl.when(side == 0)
        def _():
            first_loads[0].wait()
            first_loads[1].wait()
            first_loads[2].wait()

        values = x_buf[...].astype(F32)
        put_squares(values, 2)
        mixed = jnp.dot((values * again[...]).astype(BF), wqkv[...], preferred_element_type=F32)
        for part in range(6):
            stage[pl.ds(part, ROWS, stride=8), :] = mixed[:, HD * part:HD * (part + 1)]
        column = jnp.broadcast_to(jnp.sum(values * values, axis=1, keepdims=True), (ROWS, HD))
        rounded = column.astype(BF).astype(F32)
        stage[pl.ds(6, ROWS, stride=8), :] = rounded
        stage[pl.ds(7, ROWS, stride=8), :] = column - rounded
        send1[...] = stage[...].astype(BF).reshape(SHARDS, 16, HD)
        recv1[s] = send1[s]

        @pl.when(side == 0)
        def _():
            pl.semaphore_wait(barrier, SHARDS)

        def go1(d):
            to = shard_peer(d)
            remote(send1.at[to], recv1.at[s], send1_sem, recv1_sem, (side, to, t)).start()

        loop(1, SHARDS, go1)
        loop(1, SHARDS, lambda d: send_squares(2, d))

        @pl.when(side == 0)
        def _():
            own_loads[2].wait()
            pushes[0].start()
            first_loads[3].wait()
            first_loads[4].wait()
            turn_keys()

        lens_here = [lens[2 * s + i] for i in range(2)]
        upper_row = lax.broadcasted_iota(jnp.int32, (16, 1), 0) >= 8
        position = jnp.where(upper_row, lens_here[1], lens_here[0])
        angle = position.astype(F32) * freq[...]
        cosine = jnp.cos(angle)
        sine = jnp.where(lane < HD // 2, -jnp.sin(angle), jnp.sin(angle))

        wait_bytes(recv1.at[pl.ds(0, SHARDS - 1)], recv1_sem)
        own = jnp.sum(recv1[...].astype(F32), axis=0)
        squares = jnp.concatenate(
            [jnp.broadcast_to(own[8 * i + 6:8 * i + 7] + own[8 * i + 7:8 * i + 8], (8, HD)) for i in range(2)], axis=0)
        own = own * lax.rsqrt(squares / D + EPSILON)
        rotated = own * cosine + pltpu.roll(own, HD // 2, 1) * sine
        rotated = rotated.astype(BF).astype(F32)
        own_values = own.astype(BF).astype(F32)
        new_key = jnp.concatenate(
            [jnp.broadcast_to(rotated[8 * i + 4:8 * i + 5], (8, HD)) for i in range(2)], axis=0)
        new_value = jnp.concatenate(
            [jnp.broadcast_to(own_values[8 * i + 5:8 * i + 6], (8, HD)) for i in range(2)], axis=0)
        own_score = jnp.sum(rotated * new_key, axis=1, keepdims=True) * HD ** (-0.5)
        both = jnp.concatenate(
            [jnp.where(upper_row, 0.0, rotated), jnp.where(upper_row, rotated, 0.0)], axis=1).astype(BF)

        tops, sums, parts = [], [], []
        for c in range(CTX // CHUNK):
            scores = jnp.dot(both, keys_t[:, CHUNK * c:CHUNK * (c + 1)], preferred_element_type=F32) * HD ** (-0.5)
            at = lax.broadcasted_iota(jnp.int32, (16, CHUNK), 1) + CHUNK * c
            scores = jnp.where(at < position, scores, -1e30)
            chunk_top = jnp.maximum(jnp.max(scores, axis=1, keepdims=True), own_score)
            weights = jnp.exp(scores - chunk_top)
            tops.append(chunk_top)
            sums.append(jnp.sum(weights, axis=1, keepdims=True))
            parts.append(jnp.dot(
                weights.astype(BF), vbuf[CHUNK * c:CHUNK * (c + 1), :], preferred_element_type=F32))
        top = functools.reduce(jnp.maximum, tops)
        own_weight = jnp.exp(own_score - top)
        total, mixed_values = own_weight, 0.0
        for chunk_top, chunk_sum, part in zip(tops, sums, parts):
            share = jnp.exp(chunk_top - top)
            total = total + share * chunk_sum
            mixed_values = mixed_values + share * part
        mixed_values = jnp.concatenate([mixed_values[:8, :HD], mixed_values[8:, HD:]], axis=0)
        mixed_values = mixed_values + own_weight.astype(BF).astype(F32) * new_value
        heads = mixed_values / total
        heads = jnp.concatenate([heads[0:4], heads[8:12]], axis=0).astype(BF)
        send2[...] = heads

        @pl.when(side == 1)
        def _():
            recv2[1, s] = heads

        @pl.when(side == 0)
        def _():
            remote(send2, recv2.at[side, s], send2_sem, recv2_sem.at[side], mate).start()

        loop(1, SHARDS, lambda d: remote(
            send2, recv2.at[side, s], send2_sem, recv2_sem.at[side], (1, shard_peer(d), t)).start())
        scale_ref[0:1, :] = squares_factor(2)[:, :ROWS]

    def prepare(slot):
        for load in gu_loads:
            load.wait()
        out_row = lax.broadcasted_iota(jnp.int32, (512, 512), 0)
        in_row = lax.broadcasted_iota(jnp.int32, (512, 512), 1)
        wanted = jnp.where(out_row < 256, 2 * out_row, 2 * (out_row - 256) + 1)
        pick = jnp.where(in_row == wanted, 1.0, 0.0).astype(BF)

        def one(o):
            raw = jnp.concatenate([graw[2 * o].reshape(512, HD), graw[2 * o + 1].reshape(512, HD)], axis=1)
            apart = jnp.dot(pick, raw, preferred_element_type=F32).astype(BF)
            for part in range(4):
                wgu[slot, o, :, HD * part:HD * (part + 1)] = apart[
                    256 * (part % 2):256 * (part % 2 + 1), HD * (part // 2):HD * (part // 2 + 1)]

        loop(0, OWNERS, one)

    owner = 2 * (s // 4) + s % 4 - 1
    owns = (s % 4 >= 1) & (s % 4 <= 2) & (owner < OWNERS)

    def layer(l):
        @pl.when(l == 0)
        def _():
            wait_bytes(wout.at[0], push_recv.at[0])
            wait_bytes(recv2.at[0], recv2_sem.at[0])

        @pl.when(l == 1)
        def _():
            own_loads[2].wait()
            wait_bytes(recv2.at[1, pl.ds(0, SHARDS - 1)], recv2_sem.at[1])

        heads_f32[...] = recv2[l].astype(F32).reshape(8 * SHARDS, HD)
        gathered = jnp.concatenate(
            [heads_f32[pl.ds(g, ROWS, stride=4), :] for g in range(4)], axis=1).astype(BF)
        projected = jnp.dot(gathered, wout[l], preferred_element_type=F32).astype(BF)
        send3[l] = projected
        recv3[l, t] = projected
        loop(1, TPS, lambda d: remote(
            send3.at[l], recv3.at[l, t], send_sem.at[l, 0], recv_sem.at[l, 0], (1, s, tp_peer(d))).start())

        @pl.when(l == 0)
        def _():
            own_loads[0].wait()

        @pl.when(l == 1)
        def _():
            wait_bytes(fgain.at[1], push_recv.at[1])
            wait_bytes(wgu.at[1], push_recv.at[3])

        wait_bytes(recv3.at[l, pl.ds(0, TPS - 1)], recv_sem.at[l, 0])
        after = (x_buf[...].astype(F32) + jnp.sum(recv3[l].astype(F32), axis=0)).astype(BF)
        a_buf[...] = after
        values = after.astype(F32)
        put_squares(values, l)
        scaled = (values * fgain[l]).astype(BF)

        for part in range(2):
            for d in range(OWNERS):
                o = lax.rem(jnp.where(owns, owner + 1, s) + d, OWNERS)
                both = jnp.dot(scaled, wgu[l, o, :, 256 * part:256 * (part + 1)], preferred_element_type=F32).astype(BF)
                send4[l, part, o] = both
                send = remote(send4.at[l, part, o], recv4.at[l, part, s], send_sem.at[l, 1 + part],
                              recv_sem.at[l, 1 + part], (1, 4 * (o // 2) + 1 + o % 2, t))
                if d < OWNERS - 1:
                    send.start()
                else:
                    pl.when(jnp.logical_not(owns))(send.start)

                    @pl.when(owns)
                    def _():
                        recv4[l, part, s] = both

            if part == 0:
                loop(1, SHARDS, lambda d: send_squares(l, d))

        pl.when(l == 0)(turn_keys)
        factor = squares_factor(l)
        column = jnp.sum(jnp.where(diagonal, factor, 0.0), axis=1, keepdims=True)

        @pl.when(owns)
        def _():
            for part in range(2):
                wait_bytes(recv4.at[l, part, pl.ds(0, SHARDS - 1)], recv_sem.at[l, 1 + part])
                both = jnp.sum(recv4[l, part].astype(F32), axis=0) * column
                gate, up = both[:, :HD], both[:, HD:]
                hidden = (gate / (1.0 + jnp.exp(-gate)) * up).astype(BF)
                send5[l, part] = hidden
                recv5[l, owner, part] = hidden
                loop(1, SHARDS, lambda d: remote(
                    send5.at[l, part], recv5.at[l, owner, part], send_sem.at[l, 3], recv_sem.at[l, 3],
                    (1, shard_peer(d), t)).start())

        @pl.when(l == 0)
        def _():
            scale_ref[1:2, :] = factor[:, :ROWS]
            own_loads[1].wait()

        @pl.when(l == 1)
        def _():
            end_scale[...] = factor
            remote(end_scale, end_scale, end_send.at[1], end_recv.at[1], mate).start()
            remote(a_buf, a_buf, end_send.at[0], end_recv.at[0], mate).start()
            wait_bytes(wdn.at[1], push_recv.at[2])

        @pl.when(owns)
        def _():
            wait_bytes(recv5.at[l, pl.ds(0, OWNERS - 1)], recv_sem.at[l, 3])

        @pl.when(jnp.logical_not(owns))
        def _():
            wait_bytes(recv5.at[l], recv_sem.at[l, 3])

        hidden_all = jnp.concatenate([recv5[l, o, part] for o in range(OWNERS) for part in range(2)], axis=1)
        partial = jnp.dot(hidden_all, wdn[l], preferred_element_type=F32).astype(BF)
        send6[l] = partial

        @pl.when(l == 0)
        def _():
            recv6[t] = partial
            loop(1, TPS, lambda d: remote(
                send6.at[l], recv6.at[t], send_sem.at[l, 4], recv6_sem, (1, s, tp_peer(d))).start())
            wait_bytes(recv6.at[pl.ds(0, TPS - 1)], recv6_sem)
            result = (a_buf[...].astype(F32) + jnp.sum(recv6[...].astype(F32), axis=0)).astype(BF)
            x_buf[...] = result
            out_ref[...] = result

        @pl.when(l == 1)
        def _():
            loop(0, TPS, lambda d: remote(
                send6.at[l], recv6.at[t], send_sem.at[l, 4], recv6_sem, (0, s, tp_peer(d))).start())

    @pl.when(side == 1)
    def _():
        prepare(0)
        for load in first_loads:
            load.wait()
        pl.semaphore_wait(barrier, SHARDS - 1 + TPS - 1 + TPS)

    def step(l):
        pl.when(side == l)(attention)

        @pl.when(side == 1)
        def _():
            layer(l)

    loop(0, 2, step)

    wait_bytes(ss_recv.at[2, pl.ds(0, SHARDS - 1)], ss_send_sem.at[2])
    wait_bytes(recv1.at[pl.ds(0, SHARDS - 1)], send1_sem)

    @pl.when(side == 0)
    def _():
        prepare(1)
        for push in pushes[1:]:
            push.start()
        wait_bytes(recv2.at[0], send2_sem)
        for push in pushes:
            push.wait_send()
        wait_bytes(end_scale, end_recv.at[1])
        scale_ref[1:2, :] = end_scale[:, :ROWS]
        wait_bytes(a_buf, end_recv.at[0])
        wait_bytes(recv6, recv6_sem)
        out_ref[...] = (a_buf[...].astype(F32) + jnp.sum(recv6[...].astype(F32), axis=0)).astype(BF)

    @pl.when(side == 1)
    def _():
        wait_bytes(recv2.at[1, pl.ds(0, SHARDS - 1)], send2_sem)

        def sent(l):
            wait_bytes(ss_recv.at[l, pl.ds(0, SHARDS - 1)], ss_send_sem.at[l])
            wait_bytes(recv3.at[l, pl.ds(0, TPS - 1)], send_sem.at[l, 0])

            for part in range(2):
                @pl.when(owns)
                def _():
                    wait_bytes(recv4.at[l, part, pl.ds(0, OWNERS - 1)], send_sem.at[l, 1 + part])

                @pl.when(jnp.logical_not(owns))
                def _():
                    wait_bytes(recv4.at[l, part, pl.ds(0, OWNERS)], send_sem.at[l, 1 + part])

            @pl.when(owns)
            def _():
                wait_bytes(recv4.at[l, 0, pl.ds(0, SHARDS - 1)], send_sem.at[l, 3])

        loop(0, 2, sent)
        wait_bytes(recv6.at[pl.ds(0, TPS - 1)], send_sem.at[0, 4])
        wait_bytes(recv6, send_sem.at[1, 4])
        wait_bytes(a_buf, end_send.at[0])
        wait_bytes(end_scale, end_send.at[1])


def body(tokens, lengths, kv_cache, attn_gain, qkv_weight, out_weight, ffn_gain, gate_up, down_weight):
    freqs = (ROPE_BASE ** (-np.arange(HD // 2, dtype=np.float64) * 2.0 / HD)).astype(np.float32)
    freqs = jnp.asarray(np.concatenate([freqs, freqs])[None])
    vmem = pl.BlockSpec(memory_space=pltpu.VMEM)
    hbm = pl.BlockSpec(memory_space=pltpu.HBM)
    dma = pltpu.SemaphoreType.DMA
    out, scales = pl.pallas_call(
        kernel,
        out_shape=(pltpu.VMEM((ROWS, 256), BF), pltpu.VMEM((2, ROWS), F32)),
        in_specs=[hbm] * 10,
        out_specs=(vmem, vmem),
        scratch_shapes=[
            pltpu.SMEM((ROWS,), jnp.int32),
            pltpu.VMEM((1, 256), F32), pltpu.VMEM((2, 1, 256), F32), pltpu.VMEM((1, HD), F32),
            pltpu.VMEM((CTX, 2 * HD), BF), pltpu.VMEM((CTX, 2 * HD), BF), pltpu.VMEM((2 * HD, CTX), BF),
            pltpu.VMEM((256, 768), BF), pltpu.VMEM((2, 512, 256), BF),
            pltpu.VMEM((TILES, 256, 2, HD), BF), pltpu.VMEM((2, OWNERS, 256, 512), BF),
            pltpu.VMEM((2, TILES * HD, 256), BF),
            pltpu.VMEM((ROWS, 256), BF), pltpu.VMEM((ROWS, 256), BF),
            pltpu.VMEM((3, 1, HD), F32), pltpu.VMEM((3, SHARDS, 1, HD), F32),
            pltpu.VMEM((16 * SHARDS, HD), F32), pltpu.VMEM((SHARDS, 16, HD), BF), pltpu.VMEM((SHARDS, 16, HD), BF),
            pltpu.VMEM((8, HD), BF), pltpu.VMEM((2, SHARDS, 8, HD), BF), pltpu.VMEM((8 * SHARDS, HD), F32),
            pltpu.VMEM((2, ROWS, 256), BF), pltpu.VMEM((2, TPS, ROWS, 256), BF),
            pltpu.VMEM((2, 2, OWNERS, ROWS, 256), BF), pltpu.VMEM((2, 2, SHARDS, ROWS, 256), BF),
            pltpu.VMEM((2, 2, ROWS, HD), BF), pltpu.VMEM((2, OWNERS, 2, ROWS, HD), BF),
            pltpu.VMEM((2, ROWS, 256), BF), pltpu.VMEM((TPS, ROWS, 256), BF),
            pltpu.VMEM((1, HD), F32),
            dma((12,)), dma((TILES,)), dma((3,)), dma((3,)), dma, dma, dma, dma((2,)),
            dma((2, 5)), dma((2, 4)), dma, dma((4,)), dma((4,)), dma((2,)), dma((2,)),
        ],
        compiler_params=pltpu.CompilerParams(
            collective_id=0, has_side_effects=True, vmem_limit_bytes=63 * 1024 * 1024),
        cost_estimate=pl.CostEstimate(flops=130_000_000, bytes_accessed=7_500_000, transcendentals=70_000),
    )(*(pltpu.with_memory_space_constraint(x, pltpu.HBM) for x in (
        tokens, lengths, attn_gain, ffn_gain, freqs,
        kv_cache.reshape(2, CTX, 2 * HD), qkv_weight.reshape(256, 768), out_weight.reshape(512, 256),
        gate_up.reshape(256, 2, 1792), down_weight.reshape(1792, 256),
    )))
    return (out[None], scales[None])


def solution(mesh):
    in_specs = (
        P(None, "shard"),
        P(),
        P("side", "shard", None, "tp", None),
        P("side", "shard"),
        P("side", "shard", "tp", None),
        P("side", "tp", None, "shard"),
        P("side", "shard"),
        P("side", "shard", None, "tp"),
        P("side", "tp", "shard"),
    )
    out_specs = (P("side", None, "shard"), P("side", None, None))
    return jax.shard_map(body, mesh=mesh, in_specs=in_specs, out_specs=out_specs, check_vma=False)
```

```python
import functools

import jax
import jax.numpy as jnp
import numpy as np
from jax import lax
from jax.experimental import pallas as pl
from jax.experimental.pallas import tpu as pltpu
from jax.sharding import PartitionSpec as P

D = 4096
HD = 128
ROWS = 32
EPSILON = 1e-05
ROPE_BASE = 500000.0
SHARDS = 16
TPS = 8
TILES = 14
OWNERS = 7
CTX = 4096
CHUNK = 1024
BF = jnp.bfloat16
F32 = jnp.float32
MESH = pl.DeviceIdType.MESH


def nt_dot(a, b):
    return lax.dot_general(a, b, (((1,), (1,)), ((), ())), preferred_element_type=F32)


def wait_bytes(ref, sem):
    pltpu.make_async_copy(ref, ref, sem).wait()


def remote(src, dst, ssem, rsem, device):
    return pltpu.make_async_remote_copy(
        src_ref=src, dst_ref=dst, send_sem=ssem, recv_sem=rsem, device_id=device, device_id_type=MESH)


def kernel(
    tok_hbm, lens_hbm, again_hbm, fgain_hbm, freq_hbm, cache_hbm, wqkv_hbm, wout_hbm, wgu_hbm, wdn_hbm,
    out_ref, scale_ref,
    lens, again, fgain, freq,
    kbuf, vbuf, keys_t, wqkv, wout, graw, wgu, wdn,
    x_buf, a_buf,
    ss_send, ss_recv, stage, send1, recv1, send2, recv2, heads_f32,
    send3, recv3, send4, recv4, send5, recv5, send6, recv6, end_scale,
    load_sem, gu_sem, ss_send_sem, ss_recv_sem, send1_sem, recv1_sem, send2_sem, recv2_sem,
    send_sem, recv_sem, recv6_sem, push_send, push_recv, end_send, end_recv,
):
    side = lax.axis_index("side")
    s = lax.axis_index("shard")
    t = lax.axis_index("tp")
    mate = (1 - side, s, t)

    def shard_peer(d):
        return lax.rem(s + d, SHARDS)

    def tp_peer(d):
        return lax.rem(t + d, TPS)

    barrier = pltpu.get_barrier_semaphore()

    def greet(device):
        pl.semaphore_signal(barrier, inc=1, device_id=device, device_id_type=MESH)

    def loop(start, stop, step):
        def go(d, carry):
            step(d)
            return carry

        lax.fori_loop(start, stop, go, 0)

    @pl.when(side == 0)
    def _():
        loop(1, SHARDS, lambda d: greet((0, shard_peer(d), t)))
        loop(0, TPS, lambda d: greet((1, s, tp_peer(d))))

    @pl.when(side == 1)
    def _():
        greet(mate)
        loop(1, SHARDS, lambda d: greet((1, shard_peer(d), t)))
        loop(1, TPS, lambda d: greet((1, s, tp_peer(d))))

    first_loads = [
        pltpu.make_async_copy(tok_hbm, x_buf, load_sem.at[0]),
        pltpu.make_async_copy(again_hbm, again, load_sem.at[1]),
        pltpu.make_async_copy(wqkv_hbm, wqkv, load_sem.at[2]),
        pltpu.make_async_copy(lens_hbm, lens, load_sem.at[3]),
        pltpu.make_async_copy(freq_hbm, freq, load_sem.at[4]),
    ]
    cache_loads = []
    for i in range(2):
        cache_loads.append(pltpu.make_async_copy(
            cache_hbm.at[i, :, pl.ds(0, HD)], kbuf.at[:, pl.ds(HD * i, HD)], load_sem.at[5 + i]))
        cache_loads.append(pltpu.make_async_copy(
            cache_hbm.at[i, :, pl.ds(HD, HD)], vbuf.at[:, pl.ds(HD * i, HD)], load_sem.at[7 + i]))
    own_loads = [
        pltpu.make_async_copy(fgain_hbm, fgain.at[0], load_sem.at[9]),
        pltpu.make_async_copy(wdn_hbm, wdn.at[0], load_sem.at[10]),
        pltpu.make_async_copy(wout_hbm, wout.at[side], load_sem.at[11]),
    ]
    gu_loads = [
        pltpu.make_async_copy(wgu_hbm.at[:, :, pl.ds(HD * j, HD)], graw.at[j], gu_sem.at[j]) for j in range(TILES)
    ]
    for load in first_loads:
        load.start()
    own_loads[2].start()

    @pl.when(side == 0)
    def _():
        for load in cache_loads:
            load.start()

    for load in gu_loads:
        load.start()

    @pl.when(side == 1)
    def _():
        for load in own_loads[:2]:
            load.start()
        for load in cache_loads:
            load.start()

    pushes = [
        remote(wout.at[0], wout.at[0], push_send.at[0], push_recv.at[0], mate),
        remote(fgain_hbm, fgain.at[1], push_send.at[1], push_recv.at[1], mate),
        remote(wdn_hbm, wdn.at[1], push_send.at[2], push_recv.at[2], mate),
        remote(wgu.at[1], wgu.at[1], push_send.at[3], push_recv.at[3], mate),
    ]

    diagonal = lax.broadcasted_iota(jnp.int32, (ROWS, HD), 0) == lax.broadcasted_iota(jnp.int32, (ROWS, HD), 1)
    lane = lax.broadcasted_iota(jnp.int32, (1, HD), 1)

    def put_squares(values, which):
        column = jnp.sum(values * values, axis=1, keepdims=True)
        row = jnp.sum(jnp.where(diagonal, column, 0.0), axis=0, keepdims=True)
        ss_send[which] = row
        ss_recv[which, s] = row

    def send_squares(which, d):
        remote(ss_send.at[which], ss_recv.at[which, s], ss_send_sem.at[which], ss_recv_sem.at[which],
               (side, shard_peer(d), t)).start()

    def squares_factor(which):
        wait_bytes(ss_recv.at[which, pl.ds(0, SHARDS - 1)], ss_recv_sem.at[which])
        return lax.rsqrt(jnp.sum(ss_recv[which], axis=0) / D + EPSILON)

    def turn_keys():
        for load in cache_loads:
            load.wait()
        eye = jnp.where(
            lax.broadcasted_iota(jnp.int32, (256, 256), 0) == lax.broadcasted_iota(jnp.int32, (256, 256), 1),
            1.0, 0.0).astype(BF)

        def turn(c):
            at = pl.ds(pl.multiple_of(512 * c, 512), 512)
            keys_t[:, at] = nt_dot(eye, kbuf[at, :]).astype(BF)

        loop(0, CTX // 512, turn)

    def attention():
        @pl.when(side == 0)
        def _():
            first_loads[0].wait()
            first_loads[1].wait()
            first_loads[2].wait()

        values = x_buf[...].astype(F32)
        mixed = jnp.dot((values * again[...]).astype(BF), wqkv[...], preferred_element_type=F32)
        for part in range(6):
            stage[pl.ds(part, ROWS, stride=8), :] = mixed[:, HD * part:HD * (part + 1)]
        column = jnp.broadcast_to(jnp.sum(values * values, axis=1, keepdims=True), (ROWS, HD))
        rounded = column.astype(BF).astype(F32)
        stage[pl.ds(6, ROWS, stride=8), :] = rounded
        stage[pl.ds(7, ROWS, stride=8), :] = column - rounded
        send1[...] = stage[...].astype(BF).reshape(SHARDS, 16, HD)
        recv1[s] = send1[s]

        @pl.when(side == 0)
        def _():
            pl.semaphore_wait(barrier, SHARDS)

        def go1(d):
            to = shard_peer(d)
            remote(send1.at[to], recv1.at[s], send1_sem, recv1_sem, (side, to, t)).start()

        loop(1, SHARDS, go1)
        put_squares(values, 2)
        loop(1, SHARDS, lambda d: send_squares(2, d))

        @pl.when(side == 0)
        def _():
            own_loads[2].wait()
            pushes[0].start()
            first_loads[3].wait()
            first_loads[4].wait()
            turn_keys()

        lens_here = [lens[2 * s + i] for i in range(2)]
        upper_row = lax.broadcasted_iota(jnp.int32, (16, 1), 0) >= 8
        position = jnp.where(upper_row, lens_here[1], lens_here[0])
        angle = position.astype(F32) * freq[...]
        cosine = jnp.cos(angle)
        sine = jnp.where(lane < HD // 2, -jnp.sin(angle), jnp.sin(angle))

        wait_bytes(recv1.at[pl.ds(0, SHARDS - 1)], recv1_sem)
        own = jnp.sum(recv1[...].astype(F32), axis=0)
        squares = jnp.concatenate(
            [jnp.broadcast_to(own[8 * i + 6:8 * i + 7] + own[8 * i + 7:8 * i + 8], (8, HD)) for i in range(2)], axis=0)
        own = own * lax.rsqrt(squares / D + EPSILON)
        rotated = own * cosine + pltpu.roll(own, HD // 2, 1) * sine
        rotated = rotated.astype(BF).astype(F32)
        own_values = own.astype(BF).astype(F32)
        new_key = jnp.concatenate(
            [jnp.broadcast_to(rotated[8 * i + 4:8 * i + 5], (8, HD)) for i in range(2)], axis=0)
        new_value = jnp.concatenate(
            [jnp.broadcast_to(own_values[8 * i + 5:8 * i + 6], (8, HD)) for i in range(2)], axis=0)
        own_score = jnp.sum(rotated * new_key, axis=1, keepdims=True) * HD ** (-0.5)
        both = jnp.concatenate(
            [jnp.where(upper_row, 0.0, rotated), jnp.where(upper_row, rotated, 0.0)], axis=1).astype(BF)

        tops, sums, parts = [], [], []
        for c in range(CTX // CHUNK):
            scores = jnp.dot(both, keys_t[:, CHUNK * c:CHUNK * (c + 1)], preferred_element_type=F32) * HD ** (-0.5)
            at = lax.broadcasted_iota(jnp.int32, (16, CHUNK), 1) + CHUNK * c
            scores = jnp.where(at < position, scores, -1e30)
            chunk_top = jnp.maximum(jnp.max(scores, axis=1, keepdims=True), own_score)
            weights = jnp.exp(scores - chunk_top)
            tops.append(chunk_top)
            sums.append(jnp.sum(weights, axis=1, keepdims=True))
            parts.append(jnp.dot(
                weights.astype(BF), vbuf[CHUNK * c:CHUNK * (c + 1), :], preferred_element_type=F32))
        top = functools.reduce(jnp.maximum, tops)
        own_weight = jnp.exp(own_score - top)
        total, mixed_values = own_weight, 0.0
        for chunk_top, chunk_sum, part in zip(tops, sums, parts):
            share = jnp.exp(chunk_top - top)
            total = total + share * chunk_sum
            mixed_values = mixed_values + share * part
        mixed_values = jnp.concatenate([mixed_values[:8, :HD], mixed_values[8:, HD:]], axis=0)
        mixed_values = mixed_values + own_weight.astype(BF).astype(F32) * new_value
        heads = mixed_values / total
        heads = jnp.concatenate([heads[0:4], heads[8:12]], axis=0).astype(BF)
        send2[...] = heads

        @pl.when(side == 1)
        def _():
            recv2[1, s] = heads

        @pl.when(side == 0)
        def _():
            remote(send2, recv2.at[side, s], send2_sem, recv2_sem.at[side], mate).start()

        loop(1, SHARDS, lambda d: remote(
            send2, recv2.at[side, s], send2_sem, recv2_sem.at[side], (1, shard_peer(d), t)).start())
        scale_ref[0:1, :] = squares_factor(2)[:, :ROWS]

    def prepare(slot):
        for load in gu_loads:
            load.wait()
        out_row = lax.broadcasted_iota(jnp.int32, (512, 512), 0)
        in_row = lax.broadcasted_iota(jnp.int32, (512, 512), 1)
        wanted = jnp.where(out_row < 256, 2 * out_row, 2 * (out_row - 256) + 1)
        pick = jnp.where(in_row == wanted, 1.0, 0.0).astype(BF)

        def one(o):
            raw = jnp.concatenate([graw[2 * o].reshape(512, HD), graw[2 * o + 1].reshape(512, HD)], axis=1)
            apart = jnp.dot(pick, raw, preferred_element_type=F32).astype(BF)
            for part in range(4):
                wgu[slot, o, :, HD * part:HD * (part + 1)] = apart[
                    256 * (part % 2):256 * (part % 2 + 1), HD * (part // 2):HD * (part // 2 + 1)]

        loop(0, OWNERS, one)

    owner = 2 * (s // 4) + s % 4 - 1
    owns = (s % 4 >= 1) & (s % 4 <= 2) & (owner < OWNERS)

    def layer(l):
        @pl.when(l == 0)
        def _():
            wait_bytes(wout.at[0], push_recv.at[0])
            wait_bytes(recv2.at[0], recv2_sem.at[0])

        @pl.when(l == 1)
        def _():
            own_loads[2].wait()
            wait_bytes(recv2.at[1, pl.ds(0, SHARDS - 1)], recv2_sem.at[1])

        heads_f32[...] = recv2[l].astype(F32).reshape(8 * SHARDS, HD)
        gathered = jnp.concatenate(
            [heads_f32[pl.ds(g, ROWS, stride=4), :] for g in range(4)], axis=1).astype(BF)
        projected = jnp.dot(gathered, wout[l], preferred_element_type=F32).astype(BF)
        send3[l] = projected
        recv3[l, t] = projected
        loop(1, TPS, lambda d: remote(
            send3.at[l], recv3.at[l, t], send_sem.at[l, 0], recv_sem.at[l, 0], (1, s, tp_peer(d))).start())

        @pl.when(l == 0)
        def _():
            own_loads[0].wait()

        @pl.when(l == 1)
        def _():
            wait_bytes(fgain.at[1], push_recv.at[1])
            wait_bytes(wgu.at[1], push_recv.at[3])

        wait_bytes(recv3.at[l, pl.ds(0, TPS - 1)], recv_sem.at[l, 0])
        after = (x_buf[...].astype(F32) + jnp.sum(recv3[l].astype(F32), axis=0)).astype(BF)
        a_buf[...] = after
        values = after.astype(F32)
        scaled = (values * fgain[l]).astype(BF)

        for part in range(2):
            for d in range(OWNERS):
                o = lax.rem(jnp.where(owns, owner + 1, s) + d, OWNERS)
                both = jnp.dot(scaled, wgu[l, o, :, 256 * part:256 * (part + 1)], preferred_element_type=F32).astype(BF)
                send4[l, part, o] = both
                send = remote(send4.at[l, part, o], recv4.at[l, part, s], send_sem.at[l, 1 + part],
                              recv_sem.at[l, 1 + part], (1, 4 * (o // 2) + 1 + o % 2, t))
                if d < OWNERS - 1:
                    send.start()
                else:
                    pl.when(jnp.logical_not(owns))(send.start)

                    @pl.when(owns)
                    def _():
                        recv4[l, part, s] = both

            if part == 0:
                put_squares(values, l)
                loop(1, SHARDS, lambda d: send_squares(l, d))

        pl.when(l == 0)(turn_keys)
        factor = squares_factor(l)
        column = jnp.sum(jnp.where(diagonal, factor, 0.0), axis=1, keepdims=True)

        @pl.when(owns)
        def _():
            for part in range(2):
                wait_bytes(recv4.at[l, part, pl.ds(0, SHARDS - 1)], recv_sem.at[l, 1 + part])
                both = jnp.sum(recv4[l, part].astype(F32), axis=0) * column
                gate, up = both[:, :HD], both[:, HD:]
                hidden = (gate / (1.0 + jnp.exp(-gate)) * up).astype(BF)
                send5[l, part] = hidden
                recv5[l, owner, part] = hidden
                loop(1, SHARDS, lambda d: remote(
                    send5.at[l, part], recv5.at[l, owner, part], send_sem.at[l, 3], recv_sem.at[l, 3],
                    (1, shard_peer(d), t)).start())

        @pl.when(l == 0)
        def _():
            scale_ref[1:2, :] = factor[:, :ROWS]
            own_loads[1].wait()

        @pl.when(l == 1)
        def _():
            end_scale[...] = factor
            remote(end_scale, end_scale, end_send.at[1], end_recv.at[1], mate).start()
            remote(a_buf, a_buf, end_send.at[0], end_recv.at[0], mate).start()
            wait_bytes(wdn.at[1], push_recv.at[2])

        @pl.when(owns)
        def _():
            wait_bytes(recv5.at[l, pl.ds(0, OWNERS - 1)], recv_sem.at[l, 3])

        @pl.when(jnp.logical_not(owns))
        def _():
            wait_bytes(recv5.at[l], recv_sem.at[l, 3])

        hidden_all = jnp.concatenate([recv5[l, o, part] for o in range(OWNERS) for part in range(2)], axis=1)
        partial = jnp.dot(hidden_all, wdn[l], preferred_element_type=F32).astype(BF)
        send6[l] = partial

        @pl.when(l == 0)
        def _():
            recv6[t] = partial
            loop(1, TPS, lambda d: remote(
                send6.at[l], recv6.at[t], send_sem.at[l, 4], recv6_sem, (1, s, tp_peer(d))).start())
            wait_bytes(recv6.at[pl.ds(0, TPS - 1)], recv6_sem)
            result = (a_buf[...].astype(F32) + jnp.sum(recv6[...].astype(F32), axis=0)).astype(BF)
            x_buf[...] = result
            out_ref[...] = result

        @pl.when(l == 1)
        def _():
            loop(0, TPS, lambda d: remote(
                send6.at[l], recv6.at[t], send_sem.at[l, 4], recv6_sem, (0, s, tp_peer(d))).start())

    @pl.when(side == 1)
    def _():
        prepare(0)
        for load in first_loads:
            load.wait()
        pl.semaphore_wait(barrier, SHARDS - 1 + TPS - 1 + TPS)

    def step(l):
        pl.when(side == l)(attention)

        @pl.when(side == 1)
        def _():
            layer(l)

    loop(0, 2, step)

    wait_bytes(ss_recv.at[2, pl.ds(0, SHARDS - 1)], ss_send_sem.at[2])
    wait_bytes(recv1.at[pl.ds(0, SHARDS - 1)], send1_sem)

    @pl.when(side == 0)
    def _():
        prepare(1)
        for push in pushes[1:]:
            push.start()
        wait_bytes(recv2.at[0], send2_sem)
        for push in pushes:
            push.wait_send()
        wait_bytes(end_scale, end_recv.at[1])
        scale_ref[1:2, :] = end_scale[:, :ROWS]
        wait_bytes(a_buf, end_recv.at[0])
        wait_bytes(recv6, recv6_sem)
        out_ref[...] = (a_buf[...].astype(F32) + jnp.sum(recv6[...].astype(F32), axis=0)).astype(BF)

    @pl.when(side == 1)
    def _():
        wait_bytes(recv2.at[1, pl.ds(0, SHARDS - 1)], send2_sem)

        def sent(l):
            wait_bytes(ss_recv.at[l, pl.ds(0, SHARDS - 1)], ss_send_sem.at[l])
            wait_bytes(recv3.at[l, pl.ds(0, TPS - 1)], send_sem.at[l, 0])

            for part in range(2):
                @pl.when(owns)
                def _():
                    wait_bytes(recv4.at[l, part, pl.ds(0, OWNERS - 1)], send_sem.at[l, 1 + part])

                @pl.when(jnp.logical_not(owns))
                def _():
                    wait_bytes(recv4.at[l, part, pl.ds(0, OWNERS)], send_sem.at[l, 1 + part])

            @pl.when(owns)
            def _():
                wait_bytes(recv4.at[l, 0, pl.ds(0, SHARDS - 1)], send_sem.at[l, 3])

        loop(0, 2, sent)
        wait_bytes(recv6.at[pl.ds(0, TPS - 1)], send_sem.at[0, 4])
        wait_bytes(recv6, send_sem.at[1, 4])
        wait_bytes(a_buf, end_send.at[0])
        wait_bytes(end_scale, end_send.at[1])


def body(tokens, lengths, kv_cache, attn_gain, qkv_weight, out_weight, ffn_gain, gate_up, down_weight):
    freqs = (ROPE_BASE ** (-np.arange(HD // 2, dtype=np.float64) * 2.0 / HD)).astype(np.float32)
    freqs = jnp.asarray(np.concatenate([freqs, freqs])[None])
    vmem = pl.BlockSpec(memory_space=pltpu.VMEM)
    hbm = pl.BlockSpec(memory_space=pltpu.HBM)
    dma = pltpu.SemaphoreType.DMA
    out, scales = pl.pallas_call(
        kernel,
        out_shape=(pltpu.VMEM((ROWS, 256), BF), pltpu.VMEM((2, ROWS), F32)),
        in_specs=[hbm] * 10,
        out_specs=(vmem, vmem),
        scratch_shapes=[
            pltpu.SMEM((ROWS,), jnp.int32),
            pltpu.VMEM((1, 256), F32), pltpu.VMEM((2, 1, 256), F32), pltpu.VMEM((1, HD), F32),
            pltpu.VMEM((CTX, 2 * HD), BF), pltpu.VMEM((CTX, 2 * HD), BF), pltpu.VMEM((2 * HD, CTX), BF),
            pltpu.VMEM((256, 768), BF), pltpu.VMEM((2, 512, 256), BF),
            pltpu.VMEM((TILES, 256, 2, HD), BF), pltpu.VMEM((2, OWNERS, 256, 512), BF),
            pltpu.VMEM((2, TILES * HD, 256), BF),
            pltpu.VMEM((ROWS, 256), BF), pltpu.VMEM((ROWS, 256), BF),
            pltpu.VMEM((3, 1, HD), F32), pltpu.VMEM((3, SHARDS, 1, HD), F32),
            pltpu.VMEM((16 * SHARDS, HD), F32), pltpu.VMEM((SHARDS, 16, HD), BF), pltpu.VMEM((SHARDS, 16, HD), BF),
            pltpu.VMEM((8, HD), BF), pltpu.VMEM((2, SHARDS, 8, HD), BF), pltpu.VMEM((8 * SHARDS, HD), F32),
            pltpu.VMEM((2, ROWS, 256), BF), pltpu.VMEM((2, TPS, ROWS, 256), BF),
            pltpu.VMEM((2, 2, OWNERS, ROWS, 256), BF), pltpu.VMEM((2, 2, SHARDS, ROWS, 256), BF),
            pltpu.VMEM((2, 2, ROWS, HD), BF), pltpu.VMEM((2, OWNERS, 2, ROWS, HD), BF),
            pltpu.VMEM((2, ROWS, 256), BF), pltpu.VMEM((TPS, ROWS, 256), BF),
            pltpu.VMEM((1, HD), F32),
            dma((12,)), dma((TILES,)), dma((3,)), dma((3,)), dma, dma, dma, dma((2,)),
            dma((2, 5)), dma((2, 4)), dma, dma((4,)), dma((4,)), dma((2,)), dma((2,)),
        ],
        compiler_params=pltpu.CompilerParams(
            collective_id=0, has_side_effects=True, vmem_limit_bytes=63 * 1024 * 1024),
        cost_estimate=pl.CostEstimate(flops=130_000_000, bytes_accessed=7_500_000, transcendentals=70_000),
    )(*(pltpu.with_memory_space_constraint(x, pltpu.HBM) for x in (
        tokens, lengths, attn_gain, ffn_gain, freqs,
        kv_cache.reshape(2, CTX, 2 * HD), qkv_weight.reshape(256, 768), out_weight.reshape(512, 256),
        gate_up.reshape(256, 2, 1792), down_weight.reshape(1792, 256),
    )))
    return (out[None], scales[None])


def solution(mesh):
    in_specs = (
        P(None, "shard"),
        P(),
        P("side", "shard", None, "tp", None),
        P("side", "shard"),
        P("side", "shard", "tp", None),
        P("side", "tp", None, "shard"),
        P("side", "shard"),
        P("side", "shard", None, "tp"),
        P("side", "tp", "shard"),
    )
    out_specs = (P("side", None, "shard"), P("side", None, None))
    return jax.shard_map(body, mesh=mesh, in_specs=in_specs, out_specs=out_specs, check_vma=False)
```
